32 devices in a mesh: grp: 2 (over y), tile: 4 (over z), date: 2 (over x), row: 2 (over core).
Axes of the slice: x: 2, y: 2, z: 4, core: 2. Of those that a mesh axis runs over, the one named last changes fastest.
Arguments:
- images: bfloat16 [16, 10, 64, 1024], P('date', None, ('grp', 'tile', 'row')), parts along dimension 2, may hold values from -6 to 6
- clouds: int32 [16, 32, 512], P('date', ('grp', 'tile', 'row')), parts along dimension 1, may hold values from 0 to 1, as said below
- day_of_year: int32 [32], P(('grp', 'date')), parts along dimension 0, may hold values from 0 to 365
- conv_first: bfloat16 [9, 64, 10], replicated, may hold values from -0.625 to 0.625
- conv_second: bfloat16 [9, 64, 64], replicated, may hold values from -0.25 to 0.25
- conv_down: bfloat16 [4, 128, 64], replicated, may hold values from -0.375 to 0.375
- conv_coarse: bfloat16 [9, 128, 128], replicated, may hold values from -0.1875 to 0.1875
- key_weight: bfloat16 [64, 128], replicated, may hold values from -0.5 to 0.5
- query_weight: float32 [16, 4], replicated
- out_weight: bfloat16 [128, 128], replicated, may hold values from -0.5 to 0.5
- up_weight: bfloat16 [4, 64, 128], replicated, may hold values from -0.5 to 0.5
- dec_weight: bfloat16 [9, 64, 128], replicated, may hold values from -0.1875 to 0.1875
- cls_weight: bfloat16 [20, 64], replicated, may hold values from -0.75 to 0.75
- cls_bias: float32 [20], replicated, may hold values from -4 to 4
Outputs:
- logits: float32 [20, 64, 1024], P(None, ('grp', 'tile', 'row'), 'date'), parts along dimension 1
The draws below stay inside these ranges and needn't reach their ends.
There are 2 independent parts, one for each index of `grp`. The reference program is written for one: setup_inputs(seed, part) draws one part's arguments, and reference() takes and returns one part's arrays. A program takes and returns all parts, laid end to end along the dimension named above; an argument that names none is the same for every part. Nothing has to cross between parts.
Inputs may be any that keep to these rules, and one draw needn't show every extreme that they name: `clouds`: every pixel of the half-resolution grid has at least one date with value 1.
All inputs are finite; a program needn't handle non-finite values.
Results may differ from the reference program's by a relative error of at most 0.008.
Values may be sent and summed in bfloat16 or wider, within the bound.
A program may use at most 192 MiB of HBM per device.

```python
import jax
import jax.numpy as jnp
from jax import lax

BANDS = 10
FINE_CH = 64
COARSE_CH = 128
HEADS = 16
KEY_DIM = 4
CLASSES = 20
WIDTH = 1024
DATES = 16
HEIGHT = 32


def draw_query_weight(key, part):
    values = jax.random.normal(key, (HEADS, KEY_DIM), jnp.float32)
    return values


def draw_clouds(key, part):
    key_bits = jax.random.fold_in(key, 11)
    key_force = jax.random.fold_in(key, 23)
    bits = jax.random.randint(key_bits, (DATES, HEIGHT // 2, WIDTH // 2), 0, 2)
    forced = jax.random.randint(key_force, (HEIGHT // 2, WIDTH // 2), 0, DATES)
    hit = (jnp.arange(DATES, dtype=jnp.int32)[:, None, None] == forced[None]).astype(jnp.int32)
    return jnp.maximum(bits, hit).astype(jnp.int32)


def place_ends(entries, stream_key, smallest, high):
    longest = entries.shape.index(max(entries.shape))
    spots = []
    for shift in (0, 1):
        where = [jax.random.randint(jax.random.fold_in(stream_key, axis), (), 0, length) for axis, length in enumerate(entries.shape)]
        where[longest] = (where[longest] + shift) % entries.shape[longest]
        spots.append(tuple(where))
    return entries.at[spots[0]].set(smallest).at[spots[1]].set(high)


def levels(stream_key, extent, pieces, smallest, largest):
    def one(axis_at, shards_of):
        heights = jax.random.uniform(jax.random.fold_in(jax.random.fold_in(stream_key, 6), axis_at), (shards_of,), jnp.float32, smallest / len(pieces), largest / len(pieces))
        return jnp.repeat(jnp.exp(heights), extent[axis_at] // shards_of).reshape((-1,) + (1,) * (len(extent) - axis_at - 1))

    loudness = one(*pieces[0])
    for cut in pieces[1:]:
        loudness = loudness * one(*cut)
    return loudness


def normal_values(stream_key, dims, width, bound, shards=(), kind=jnp.bfloat16):
    array = width * jax.random.normal(stream_key, dims, jnp.float32)
    if shards:
        array = array * levels(stream_key, dims, shards, -0.22, 0.18)
    return jnp.clip(array, -bound, bound).astype(kind)


def setup_inputs(seed: int = 0, part: int = 0) -> dict:
    key_of = jax.random.split(jax.random.key(seed), 15)
    part_keys = jax.random.split(jax.random.fold_in(key_of[14], part), 15)
    return {
        "images": normal_values(part_keys[0], (DATES, BANDS, HEIGHT, WIDTH), 1.0, 6.0, ((0, 2), (2, 8))),
        "clouds": draw_clouds(jax.random.fold_in(jax.random.fold_in(key_of[14], part), 71), part),
        "day_of_year": place_ends(jax.random.randint(part_keys[2], (DATES,), 0, 366), jax.random.fold_in(part_keys[2], 1), 0, 365).astype(jnp.int32),
        "conv_first": normal_values(key_of[3], (9, FINE_CH, BANDS), (9 * BANDS) ** -0.5, 0.625),
        "conv_second": normal_values(key_of[4], (9, FINE_CH, FINE_CH), (9 * FINE_CH) ** -0.5, 0.25),
        "conv_down": normal_values(key_of[5], (4, COARSE_CH, FINE_CH), (4 * FINE_CH) ** -0.5, 0.375),
        "conv_coarse": normal_values(key_of[6], (9, COARSE_CH, COARSE_CH), (9 * COARSE_CH) ** -0.5, 0.1875),
        "key_weight": normal_values(key_of[7], (HEADS * KEY_DIM, COARSE_CH), COARSE_CH ** -0.5, 0.5),
        "query_weight": draw_query_weight(jax.random.fold_in(key_of[14], 71), part),
        "out_weight": normal_values(key_of[9], (COARSE_CH, COARSE_CH), COARSE_CH ** -0.5, 0.5),
        "up_weight": normal_values(key_of[10], (4, FINE_CH, COARSE_CH), COARSE_CH ** -0.5, 0.5),
        "dec_weight": normal_values(key_of[11], (9, FINE_CH, 2 * FINE_CH), (18 * FINE_CH) ** -0.5, 0.1875),
        "cls_weight": normal_values(key_of[12], (CLASSES, FINE_CH), FINE_CH ** -0.5, 0.75),
        "cls_bias": normal_values(key_of[13], (CLASSES,), 1.0, 4.0, (), jnp.float32),
    }


def rms_norm(values, axis):
    return values * lax.rsqrt(lax.optimization_barrier(jnp.mean(values * values, axis=axis, keepdims=True)) + 1e-05)

def activate(values, axis):
    return jnp.maximum(rms_norm(values, axis), 0.0)

def conv_valid(padded, weight):
    row_count = padded.shape[-2] - 2
    col_count = padded.shape[-1] - 2
    source = padded.astype(jnp.float32)
    kernel = weight.astype(jnp.float32)
    result = None
    for tap_index in range(9):
        tap_row = tap_index // 3
        tap_col = tap_index % 3
        window = source[..., tap_row:tap_row + row_count, tap_col:tap_col + col_count]
        term_map = jnp.einsum('oi,...iyx->...oyx', kernel[tap_index], window)
        result = term_map if result is None else result + term_map
    return result

def pad_both(values):
    return jnp.pad(values, [(0, 0)] * (values.ndim - 2) + [(1, 1), (1, 1)])

def reference(images, clouds, day_of_year, conv_first, conv_second, conv_down, conv_coarse, key_weight, query_weight, out_weight, up_weight, dec_weight, cls_weight, cls_bias):

    def encode(image):
        first_map = activate(conv_valid(pad_both(image), conv_first), 0).astype(jnp.bfloat16)
        fine_map = activate(conv_valid(pad_both(first_map), conv_second), 0).astype(jnp.bfloat16)
        blocks = fine_map.astype(jnp.float32).reshape(FINE_CH, HEIGHT // 2, 2, WIDTH // 2, 2)
        lowered = jnp.einsum('abou,uyaxb->oyx', conv_down.astype(jnp.float32).reshape(2, 2, COARSE_CH, FINE_CH), blocks)
        lowered = activate(lowered, 0).astype(jnp.bfloat16)
        coarse_map = activate(conv_valid(pad_both(lowered), conv_coarse), 0).astype(jnp.bfloat16)
        return (fine_map, coarse_map)
    fine_maps, coarse_maps = lax.map(encode, images)
    half_ch = COARSE_CH // 2
    freqs = jnp.power(1000.0, -2.0 * jnp.arange(half_ch, dtype=jnp.float32) / COARSE_CH)
    angles = day_of_year.astype(jnp.float32)[:, None] * freqs[None, :]
    encoding = jnp.concatenate([jnp.sin(angles), jnp.cos(angles)], axis=1)
    key_f32 = key_weight.astype(jnp.float32)
    key_maps = jnp.einsum('ko,tohw->tkhw', key_f32, coarse_maps.astype(jnp.float32))
    key_maps = key_maps + jnp.dot(encoding, key_f32.T, precision=lax.Precision.HIGHEST)[:, :, None, None]
    coarse_rows = HEIGHT // 2
    coarse_cols = WIDTH // 2
    key_maps = key_maps.reshape(DATES, HEADS, KEY_DIM, coarse_rows, coarse_cols)
    scores = 0.5 * lax.optimization_barrier(jnp.sum(key_maps * query_weight[None, :, :, None, None], axis=2))
    is_valid = (clouds == 1)[:, None]
    masked = jnp.where(is_valid, scores, -1e+30)
    top = lax.optimization_barrier(jnp.max(masked, axis=0))
    expd = jnp.where(is_valid, jnp.exp(masked - top[None]), 0.0)
    attention = expd / lax.optimization_barrier(jnp.sum(expd, axis=0))[None]
    grouped = coarse_maps.astype(jnp.float32).reshape(DATES, HEADS, COARSE_CH // HEADS, coarse_rows, coarse_cols)
    aggregate = lax.optimization_barrier(jnp.sum(attention[:, :, None] * grouped, axis=0)).reshape(COARSE_CH, coarse_rows, coarse_cols).astype(jnp.bfloat16)
    coarse_out = activate(jnp.einsum('oi,ihw->ohw', out_weight.astype(jnp.float32), aggregate.astype(jnp.float32)), 0).astype(jnp.bfloat16)
    attn_fine = jnp.repeat(jnp.repeat(attention, 2, axis=2), 2, axis=3)

    def accumulate(total, pair):
        weights_now, fine_now = pair
        grouped_now = fine_now.astype(jnp.float32).reshape(HEADS, FINE_CH // HEADS, HEIGHT, WIDTH)
        return (total + weights_now[:, None] * grouped_now, None)
    start_sum = jnp.zeros((HEADS, FINE_CH // HEADS, HEIGHT, WIDTH), jnp.float32)
    skip_sum, unused = lax.scan(accumulate, start_sum, (attn_fine, fine_maps))
    skip_map = skip_sum.reshape(FINE_CH, HEIGHT, WIDTH).astype(jnp.bfloat16)
    taps = jnp.einsum('koi,iyx->koyx', up_weight.astype(jnp.float32), coarse_out.astype(jnp.float32))
    taps = taps.reshape(2, 2, FINE_CH, coarse_rows, coarse_cols).transpose(2, 3, 0, 4, 1)
    up_map = taps.reshape(FINE_CH, HEIGHT, WIDTH).astype(jnp.bfloat16)
    joined = jnp.concatenate([up_map, skip_map], axis=0)
    decoded = activate(conv_valid(pad_both(joined), dec_weight), 0).astype(jnp.bfloat16)
    logits = jnp.einsum('co,oyx->cyx', cls_weight.astype(jnp.float32), decoded.astype(jnp.float32))
    return logits + cls_bias[:, None, None]
```

```python
import functools

import jax
import jax.numpy as jnp
import numpy as np
from jax import lax
from jax.experimental import pallas as pl
from jax.experimental.pallas import tpu as pltpu
from jax.sharding import PartitionSpec as P

BF = jnp.bfloat16
F32 = jnp.float32
NEG = -1e30
ROWS = ("tile", "row")


def dot(a, b):
    return lax.dot_general(a, b, (((1,), (0,)), ((), ())), preferred_element_type=F32)


def act(y):
    ms = jnp.mean(y * y, axis=1, keepdims=True)
    return jnp.maximum(y * lax.rsqrt(ms + 1e-5), 0.0)


def from_left(x):
    lane = lax.broadcasted_iota(jnp.int32, x.shape, x.ndim - 1)
    return jnp.where(lane == 0, 0.0, pltpu.roll(x, 1, x.ndim - 1))


def from_right(x):
    n = x.shape[-1]
    lane = lax.broadcasted_iota(jnp.int32, x.shape, x.ndim - 1)
    return jnp.where(lane == n - 1, 0.0, pltpu.roll(x, n - 1, x.ndim - 1))


COL = ((1, 2, 0, None), (0, 1, None, 2))


def paired(w, order):
    lines = []
    for ro in range(2):
        for po in range(2):
            line = []
            for ri in range(4):
                a = ri - ro
                for v, lo, hi in order:
                    b = COL[po][v]
                    if b is None or not 0 <= a < 3:
                        line.append(jnp.zeros((w.shape[1], hi - lo), w.dtype))
                    else:
                        line.append(w[3 * a + b, :, lo:hi])
            lines.append(jnp.concatenate(line, axis=1))
    return jnp.concatenate(lines, axis=0)


def coarse_weight(w):
    lines = []
    for ro in range(2):
        line = []
        for ri in range(4):
            a = ri - ro
            for b in (1, 0, 2):
                if 0 <= a < 3:
                    line.append(w[3 * a + b])
                else:
                    line.append(jnp.zeros(w.shape[1:], w.dtype))
        lines.append(jnp.concatenate(line, axis=1))
    return jnp.concatenate(lines, axis=0)


def regroup(w, axis, heads):
    axis = axis % w.ndim
    n = w.shape[axis] // heads
    shape = w.shape[:axis] + (heads, n) + w.shape[axis + 1:]
    return jnp.swapaxes(w.reshape(shape), axis, axis + 1).reshape(w.shape)


def encode_kernel(heads, fine_ch, coarse_ch, edge_ref, img_ref, cloud_ref, sel_ref, w1_ref, w2_ref, wd_ref, wc_ref,
                  kw_ref, kb_ref, q_ref, ml_ref, out_ref, xi, s1, s2, m_s, l_s, a_s, k_s):
    t = pl.program_id(0)
    half = xi.shape[1]
    bands = 16
    top, bottom = edge_ref[0], edge_ref[1]

    @pl.when(t == 0)
    def _():
        m_s[...] = jnp.full(m_s.shape, NEG, F32)
        l_s[...] = jnp.zeros(l_s.shape, F32)
        a_s[...] = jnp.zeros(a_s.shape, F32)
        k_s[...] = jnp.zeros(k_s.shape, F32)

    sel = sel_ref[...]
    es, os = [], []
    for q in range(2 * half // 256):
        y = dot(img_ref[0, :, 256 * q:256 * q + 256], sel)
        es.append(y[:, :128])
        os.append(y[:, 128:])
    e = jnp.concatenate(es, axis=1)
    o = jnp.concatenate(os, axis=1)
    variants = (e, o, from_left(o), from_right(e))
    for v, x in enumerate(variants):
        x = x.astype(BF)
        for r in range(12):
            xi[64 * r + bands * v:64 * r + bands * v + bands, :] = x[bands * r:bands * r + bands]
    for g in range(5):
        y = dot(w1_ref[...], xi[128 * g:128 * g + 256, :])
        y = act(y.reshape(4, fine_ch, half))
        for ro in range(2):
            k = 2 * g + ro
            e, o = y[2 * ro], y[2 * ro + 1]
            if k < 3:
                e, o = e * top, o * top
            if k > 6:
                e, o = e * bottom, o * bottom
            base = 4 * fine_ch * k
            for v, x in enumerate((e, o, from_left(o), from_right(e))):
                s1[base + fine_ch * v:base + fine_ch * (v + 1), :] = x.astype(BF)
    fines = []
    for g in range(4):
        y = dot(w2_ref[...], s1[8 * fine_ch * g:8 * fine_ch * g + 16 * fine_ch, :])
        f = act(y.reshape(4, fine_ch, half)).reshape(4 * fine_ch, half).astype(BF)
        if g in (1, 2):
            fines.append(f)
        low = act(dot(wd_ref[...], f)[None])[0]
        if g == 0:
            low = low * top
        if g == 3:
            low = low * bottom
        base = 3 * coarse_ch * g
        for v, x in enumerate((low, from_left(low), from_right(low))):
            s2[base + coarse_ch * v:base + coarse_ch * (v + 1), :] = x.astype(BF)
    y = dot(wc_ref[...], s2[...])
    coarse = act(y.reshape(2, coarse_ch, half)).reshape(2 * coarse_ch, half).astype(BF)
    km = (dot(kw_ref[...], coarse) + kb_ref[0]) * q_ref[...]
    km = km.reshape(2, km.shape[0] // (2 * heads), heads, half)
    scores = 0.5 * jnp.sum(km, axis=1)
    for rr in range(2):
        valid = cloud_ref[0, rr:rr + 1, :] == 1
        s = jnp.where(valid, scores[rr], NEG)
        m_old = m_s[rr]
        m_new = jnp.maximum(m_old, s)
        f = jnp.exp(m_old - m_new)
        p = jnp.where(valid, jnp.exp(s - m_new), 0.0)
        m_s[rr] = m_new
        l_s[rr] = l_s[rr] * f + p
        c = coarse[coarse_ch * rr:coarse_ch * (rr + 1)].reshape(-1, heads, half).astype(F32)
        a_s[rr] = a_s[rr] * f[None] + p[None] * c
        c = fines[rr].reshape(-1, heads, half).astype(F32)
        k_s[rr] = k_s[rr] * f[None] + p[None] * c

    @pl.when(t == pl.num_programs(0) - 1)
    def _():
        for rr in range(2):
            total = l_s[rr]
            ml_ref[heads * rr:heads * (rr + 1), :] = m_s[rr]
            ml_ref[heads * (2 + rr):heads * (3 + rr), :] = total
            inv = (1.0 / jnp.maximum(total, 0.5))[None]
            a = (a_s[rr] * inv).reshape(coarse_ch, half)
            out_ref[coarse_ch * rr:coarse_ch * (rr + 1), :] = a.astype(BF)
            base = 2 * coarse_ch + 4 * fine_ch * rr
            k = (k_s[rr] * inv).reshape(4 * fine_ch, half)
            out_ref[base:base + 4 * fine_ch, :] = k.astype(BF)


def combine_kernel(heads, fine_ch, coarse_ch, ml_ref, ab_ref, wo_ref, wu_ref, out_ref):
    dates = ml_ref.shape[0]
    width = ml_ref.shape[2]
    for rr in range(2):
        ms = [ml_ref[d, heads * rr:heads * (rr + 1), :] for d in range(dates)]
        top = functools.reduce(jnp.maximum, ms)
        ws = [ml_ref[d, heads * (2 + rr):heads * (3 + rr), :] * jnp.exp(ms[d] - top) for d in range(dates)]
        inv = 1.0 / functools.reduce(jnp.add, ws)
        ws = [(w * inv)[None] for w in ws]

        def mix(base, size):
            parts = [
                ws[d] * ab_ref[d, base:base + size, :].reshape(-1, heads, width).astype(F32) for d in range(dates)
            ]
            return functools.reduce(jnp.add, parts).reshape(size, width).astype(BF)

        agg = mix(coarse_ch * rr, coarse_ch)
        skip = mix(2 * coarse_ch + 4 * fine_ch * rr, 4 * fine_ch)
        co = act(dot(wo_ref[...], agg)[None])[0].astype(BF)
        up = dot(wu_ref[...], co).astype(BF)
        n = 2 * fine_ch
        for a in range(2):
            base = 2 * n * (2 * rr + a)
            out_ref[base:base + n, :] = up[n * a:n * (a + 1)]
            out_ref[base + n:base + 2 * n, :] = skip[n * a:n * (a + 1)]


def decode_kernel(fine_ch, off_ref, top_ref, mid_ref, low_ref, wdec_ref, cls_ref, bias_ref, out_ref, s3):
    width = s3.shape[1]
    n = 4 * fine_ch
    rows = mid_ref.shape[0] // n
    for k in range(rows + 2):
        if k == 0:
            x = top_ref[...]
        elif k == rows + 1:
            x = low_ref[...]
        else:
            x = mid_ref[n * (k - 1):n * k, :]
        base = 2 * n * k
        s3[base:base + n, :] = x
        x = x.astype(F32).reshape(2, 2, fine_ch, width)
        half = 2 * fine_ch
        s3[base + n:base + n + half, :] = from_left(x[:, 1].reshape(half, width)).astype(BF)
        s3[base + n + half:base + 2 * n, :] = from_right(x[:, 0].reshape(half, width)).astype(BF)
    share = out_ref.shape[2]
    src = lax.broadcasted_iota(jnp.int32, (2 * width, share), 0)
    dst = lax.broadcasted_iota(jnp.int32, (2 * width, share), 1)
    pick = (src == off_ref[0] + lax.shift_right_logical(dst, 1) + (dst & 1) * width).astype(F32).astype(BF)
    for g in range(rows // 2):
        y = dot(wdec_ref[...], s3[4 * n * g:4 * n * g + 8 * n, :])
        y = act(y.reshape(4, fine_ch, width)).astype(BF)
        for ro in range(2):
            d = jnp.concatenate([y[2 * ro], y[2 * ro + 1]], axis=1)
            d = dot(d, pick).astype(BF)
            out_ref[:, 2 * g + ro, :] = dot(cls_ref[...], d) + bias_ref[...]


VMEM = pl.BlockSpec(memory_space=pltpu.VMEM)
SMEM = pl.BlockSpec(memory_space=pltpu.SMEM)


def neighbour_shift(x, step):
    count = lax.axis_size(ROWS)
    if step > 0:
        pairs = [(i, i + 1) for i in range(count - 1)]
    else:
        pairs = [(i + 1, i) for i in range(count - 1)]
    return lax.ppermute(x, ROWS, pairs)


def body(images, clouds, day_of_year, conv_first, conv_second, conv_down, conv_coarse, key_weight, query_weight,
         out_weight, up_weight, dec_weight, cls_weight, cls_bias):
    dates, bands, rows, cols = images.shape
    half = cols // 2
    fine_ch = conv_second.shape[1]
    coarse_ch = conv_coarse.shape[1]
    heads, key_size = query_weight.shape
    classes = cls_weight.shape[0]
    groups = lax.axis_size("date")
    me = lax.axis_index("date")
    band = lax.axis_index(ROWS)
    count = lax.axis_size(ROWS)

    above = neighbour_shift(images, 1)
    below = neighbour_shift(images, -1)
    ext = jnp.concatenate([above, images, below], axis=2)
    ext = jnp.pad(jnp.transpose(ext, (0, 2, 1, 3)), ((0, 0), (0, 0), (0, 16 - bands), (0, 0)))
    ext = ext.reshape(dates, 12 * 16, cols)

    edges = jnp.stack([(band > 0).astype(F32), (band < count - 1).astype(F32)])

    sel = np.zeros((256, 256), np.float32)
    for i in range(128):
        sel[2 * i, i] = 1
        sel[2 * i + 1, 128 + i] = 1
    sel = jnp.asarray(sel, BF)

    w1 = paired(jnp.pad(conv_first, ((0, 0), (0, 0), (0, 16 - bands))), [(v, 0, 16) for v in range(4)])
    w2 = paired(regroup(conv_second, 1, heads), [(v, 0, fine_ch) for v in range(4)])
    wd = jnp.transpose(regroup(conv_down, 2, heads), (1, 0, 2)).reshape(coarse_ch, 4 * fine_ch)
    wc = coarse_weight(regroup(conv_coarse, 1, heads))
    kw = regroup(regroup(key_weight, 0, heads), 1, heads)
    zero = jnp.zeros_like(kw)
    kw2 = jnp.concatenate([jnp.concatenate([kw, zero], 1), jnp.concatenate([zero, kw], 1)], 0)
    half_ch = coarse_ch // 2
    freqs = jnp.power(1000.0, -2.0 * jnp.arange(half_ch, dtype=F32) / coarse_ch)
    angles = day_of_year.astype(F32)[:, None] * freqs[None, :]
    encoding = jnp.concatenate([jnp.sin(angles), jnp.cos(angles)], axis=1)
    kb = jnp.dot(encoding, key_weight.astype(F32).T, precision=lax.Precision.HIGHEST)
    kb = regroup(kb, 1, heads)
    kb = jnp.concatenate([kb, kb], axis=1)[:, :, None]
    qv = jnp.transpose(query_weight).reshape(-1)
    qv = jnp.concatenate([qv, qv])[:, None]

    nk = 2 * heads * key_size
    total = 2 * coarse_ch + 8 * fine_ch
    const = lambda *shape: pl.BlockSpec(shape, lambda t: (0,) * len(shape))
    ml, ab = pl.pallas_call(
        functools.partial(encode_kernel, heads, fine_ch, coarse_ch),
        grid=(dates,),
        in_specs=[
            SMEM,
            pl.BlockSpec((1, 192, cols), lambda t: (t, 0, 0)),
            pl.BlockSpec((1, 2, half), lambda t: (t, 0, 0)),
            const(256, 256),
            const(*w1.shape),
            const(*w2.shape),
            const(*wd.shape),
            const(*wc.shape),
            const(*kw2.shape),
            pl.BlockSpec((1, nk, 1), lambda t: (t, 0, 0)),
            const(nk, 1),
        ],
        out_specs=[const(4 * heads, half), const(total, half)],
        out_shape=[jax.ShapeDtypeStruct((4 * heads, half), F32), jax.ShapeDtypeStruct((total, half), BF)],
        scratch_shapes=[
            pltpu.VMEM((12 * 64, half), BF),
            pltpu.VMEM((40 * fine_ch, half), BF),
            pltpu.VMEM((12 * coarse_ch, half), BF),
            pltpu.VMEM((2, heads, half), F32),
            pltpu.VMEM((2, heads, half), F32),
            pltpu.VMEM((2, coarse_ch // heads, heads, half), F32),
            pltpu.VMEM((2, 4 * fine_ch // heads, heads, half), F32),
        ],
        compiler_params=pltpu.CompilerParams(vmem_limit_bytes=48 * 1024 * 1024),
    )(edges, ext, clouds, sel, w1, w2, wd, wc, kw2, kb, qv)

    per = half // groups
    spans = []
    for k in range(groups):
        lo = max(0, (k * per - 1) // 128)
        hi = min(half // 128 - 1, (k * per + per) // 128)
        spans.append((lo, hi))
    width = max(hi - lo + 1 for lo, hi in spans) * 128
    starts = jnp.asarray([min(lo * 128, half - width) for lo, hi in spans], jnp.int32)

    def window(x, k):
        return lax.dynamic_slice_in_dim(x, starts[k], width, 1)

    mls, abs_ = [window(ml, me)], [window(ab, me)]
    for step in range(1, groups):
        to = lax.rem(me + step, groups)
        pairs = [(i, (i + step) % groups) for i in range(groups)]
        mls.append(lax.ppermute(window(ml, to), "date", pairs))
        abs_.append(lax.ppermute(window(ab, to), "date", pairs))
    joined = pl.pallas_call(
        functools.partial(combine_kernel, heads, fine_ch, coarse_ch),
        in_specs=[VMEM] * 4,
        out_specs=VMEM,
        out_shape=jax.ShapeDtypeStruct((rows * 4 * fine_ch, width), BF),
        compiler_params=pltpu.CompilerParams(vmem_limit_bytes=48 * 1024 * 1024),
    )(jnp.stack(mls), jnp.stack(abs_), regroup(out_weight, 1, heads), up_weight.reshape(4 * fine_ch, coarse_ch))

    n = 4 * fine_ch
    top = neighbour_shift(joined[-n:], 1)
    low = neighbour_shift(joined[:n], -1)
    dec = jnp.concatenate([dec_weight[:, :, :fine_ch], regroup(dec_weight[:, :, fine_ch:], 2, heads)], axis=2)
    up_part, skip_part = (0, fine_ch), (fine_ch, 2 * fine_ch)
    wdec = paired(dec, [(0, *up_part), (1, *up_part), (0, *skip_part), (1, *skip_part),
                        (2, *up_part), (2, *skip_part), (3, *up_part), (3, *skip_part)])
    offset = (me * per - starts[me]).astype(jnp.int32).reshape(1)
    return pl.pallas_call(
        functools.partial(decode_kernel, fine_ch),
        in_specs=[SMEM] + [VMEM] * 6,
        out_specs=VMEM,
        out_shape=jax.ShapeDtypeStruct((classes, rows, cols // groups), F32),
        scratch_shapes=[pltpu.VMEM(((rows + 2) * 2 * n, width), BF)],
        compiler_params=pltpu.CompilerParams(vmem_limit_bytes=48 * 1024 * 1024),
    )(offset, top, joined, low, wdec, cls_weight, cls_bias[:, None])


def solution(mesh):
    return jax.shard_map(
        body,
        mesh=mesh,
        in_specs=(
            P("date", None, ("grp", "tile", "row"), None),
            P("date", ("grp", "tile", "row"), None),
            P(("grp", "date")),
        ) + (P(),) * 11,
        out_specs=P(None, ("grp", "tile", "row"), "date"),
        check_vma=False,
    )
```

```python
import functools

import jax
import jax.numpy as jnp
import numpy as np
from jax import lax
from jax.experimental import pallas as pl
from jax.experimental.pallas import tpu as pltpu
from jax.sharding import PartitionSpec as P

BF = jnp.bfloat16
F32 = jnp.float32
NEG = -1e30
ROWS = ("tile", "row")


def dot(a, b):
    return lax.dot_general(a, b, (((1,), (0,)), ((), ())), preferred_element_type=F32)


def act(y):
    ms = jnp.mean(y * y, axis=1, keepdims=True)
    return jnp.maximum(y * lax.rsqrt(ms + 1e-5), 0.0)


def from_left(x):
    lane = lax.broadcasted_iota(jnp.int32, x.shape, x.ndim - 1)
    return jnp.where(lane == 0, 0.0, pltpu.roll(x, 1, x.ndim - 1))


def from_right(x):
    n = x.shape[-1]
    lane = lax.broadcasted_iota(jnp.int32, x.shape, x.ndim - 1)
    return jnp.where(lane == n - 1, 0.0, pltpu.roll(x, n - 1, x.ndim - 1))


COL = ((1, 2, 0, None), (0, 1, None, 2))


def paired(tap, order):
    lines = []
    for ro in range(2):
        for po in range(2):
            line = []
            for ri in range(4):
                a = ri - ro
                for v, lo, hi in order:
                    b = COL[po][v]
                    if b is None or not 0 <= a < 3:
                        line.append(jnp.zeros((tap[0].shape[0], hi - lo), tap[0].dtype))
                    else:
                        line.append(tap[3 * a + b][:, lo:hi])
            lines.append(jnp.concatenate(line, axis=1))
    return lines


def weights_kernel(perm_f_ref, perm_c_ref, first_ref, second_ref, down_ref, coarse_ref, key_ref, out_ref, dec_ref,
                   perm_k_ref, w1_ref, w2_ref, wd_ref, wc_ref, kw_ref, wo_ref, wdec_ref):
    fine_ch = second_ref.shape[1]
    coarse_ch = coarse_ref.shape[1]
    bands = first_ref.shape[2]
    perm_f, perm_c = perm_f_ref[...], perm_c_ref[...]

    def right(w, perm):
        return lax.dot_general(w, perm, (((1,), (1,)), ((), ())), preferred_element_type=F32)

    row = lax.broadcasted_iota(jnp.int32, (bands, 256), 0)
    col = lax.broadcasted_iota(jnp.int32, (bands, 256), 1)
    for ro in range(2):
        for po in range(2):
            total = jnp.zeros((fine_ch, 256), F32)
            for ri in range(4):
                for v in range(4):
                    a, b = ri - ro, COL[po][v]
                    if b is not None and 0 <= a < 3:
                        place = (col == row + (4 * ri + v) * 16).astype(F32).astype(BF)
                        total = total + dot(first_ref[3 * a + b], place)
            base = fine_ch * (2 * ro + po)
            w1_ref[base:base + fine_ch, :] = total.astype(BF)
    taps = [dot(perm_f, second_ref[k]) for k in range(9)]
    for k, line in enumerate(paired(taps, [(v, 0, fine_ch) for v in range(4)])):
        w2_ref[fine_ch * k:fine_ch * (k + 1), :] = line.astype(BF)
    wd_ref[...] = jnp.concatenate([right(down_ref[k], perm_f) for k in range(4)], axis=1).astype(BF)
    taps = [dot(perm_c, coarse_ref[k]).astype(BF) for k in range(9)]
    for ro in range(2):
        for ri in range(4):
            for v, b in enumerate((1, 0, 2)):
                a = ri - ro
                x = taps[3 * a + b] if 0 <= a < 3 else jnp.zeros((coarse_ch, coarse_ch), BF)
                base = coarse_ch * (3 * ri + v)
                wc_ref[coarse_ch * ro:coarse_ch * (ro + 1), base:base + coarse_ch] = x
    kw = right(dot(perm_k_ref[...], key_ref[...]).astype(BF), perm_c).astype(BF)
    nk = kw.shape[0]
    kw_ref[...] = jnp.zeros(kw_ref.shape, BF)
    kw_ref[:nk, :coarse_ch] = kw
    kw_ref[nk:, coarse_ch:] = kw
    wo_ref[...] = right(out_ref[...], perm_c).astype(BF)
    taps = []
    for k in range(9):
        w = dec_ref[k]
        taps.append(jnp.concatenate([w[:, :fine_ch].astype(F32), right(w[:, fine_ch:], perm_f)], axis=1))
    up, skip = (0, fine_ch), (fine_ch, 2 * fine_ch)
    order = [(0, *up), (1, *up), (0, *skip), (1, *skip), (2, *up), (2, *skip), (3, *up), (3, *skip)]
    for k, line in enumerate(paired(taps, order)):
        wdec_ref[fine_ch * k:fine_ch * (k + 1), :] = line.astype(BF)


def regroup_matrix(n, heads):
    m = np.zeros((n, n), np.float32)
    for h in range(heads):
        for i in range(n // heads):
            m[i * heads + h, h * (n // heads) + i] = 1
    return jnp.asarray(m, BF)


def regroup(w, axis, heads):
    axis = axis % w.ndim
    n = w.shape[axis] // heads
    shape = w.shape[:axis] + (heads, n) + w.shape[axis + 1:]
    return jnp.swapaxes(w.reshape(shape), axis, axis + 1).reshape(w.shape)


def encode_kernel(heads, fine_ch, coarse_ch, edge_ref, up_ref, img_ref, dn_ref, cloud_ref, order_ref, sel_ref, w1_ref, w2_ref, wd_ref, wc_ref,
                  kw_ref, kb_ref, q_ref, ml_ref, out_ref, xi, s1, s2, m_s, l_s, a_s, k_s):
    t = pl.program_id(0)
    half = xi.shape[1]
    bands = 16
    top, bottom = edge_ref[0], edge_ref[1]

    @pl.when(t == 0)
    def _():
        m_s[...] = jnp.full(m_s.shape, NEG, F32)
        l_s[...] = jnp.zeros(l_s.shape, F32)
        a_s[...] = jnp.zeros(a_s.shape, F32)
        k_s[...] = jnp.zeros(k_s.shape, F32)

    sel = sel_ref[...]
    img = jnp.concatenate([r[0].astype(F32) for r in (up_ref, img_ref, dn_ref)], axis=0).astype(BF)
    img = dot(order_ref[...], img).astype(BF)
    es, os = [], []
    for q in range(2 * half // 256):
        y = dot(img[:, 256 * q:256 * q + 256], sel)
        es.append(y[:, :128])
        os.append(y[:, 128:])
    e = jnp.concatenate(es, axis=1)
    o = jnp.concatenate(os, axis=1)
    variants = (e, o, from_left(o), from_right(e))
    for v, x in enumerate(variants):
        x = x.astype(BF)
        for r in range(12):
            xi[64 * r + bands * v:64 * r + bands * v + bands, :] = x[bands * r:bands * r + bands]
    for g in range(5):
        y = dot(w1_ref[...], xi[128 * g:128 * g + 256, :])
        y = act(y.reshape(4, fine_ch, half))
        for ro in range(2):
            k = 2 * g + ro
            e, o = y[2 * ro], y[2 * ro + 1]
            if k < 3:
                e, o = e * top, o * top
            if k > 6:
                e, o = e * bottom, o * bottom
            base = 4 * fine_ch * k
            for v, x in enumerate((e, o, from_left(o), from_right(e))):
                s1[base + fine_ch * v:base + fine_ch * (v + 1), :] = x.astype(BF)
    fines = []
    for g in range(4):
        y = dot(w2_ref[...], s1[8 * fine_ch * g:8 * fine_ch * g + 16 * fine_ch, :])
        f = act(y.reshape(4, fine_ch, half)).reshape(4 * fine_ch, half).astype(BF)
        if g in (1, 2):
            fines.append(f)
        low = act(dot(wd_ref[...], f)[None])[0]
        if g == 0:
            low = low * top
        if g == 3:
            low = low * bottom
        base = 3 * coarse_ch * g
        for v, x in enumerate((low, from_left(low), from_right(low))):
            s2[base + coarse_ch * v:base + coarse_ch * (v + 1), :] = x.astype(BF)
    y = dot(wc_ref[...], s2[...])
    coarse = act(y.reshape(2, coarse_ch, half)).reshape(2 * coarse_ch, half).astype(BF)
    km = (dot(kw_ref[...], coarse) + kb_ref[0]) * q_ref[...]
    km = km.reshape(2, km.shape[0] // (2 * heads), heads, half)
    scores = 0.5 * jnp.sum(km, axis=1)
    for rr in range(2):
        valid = cloud_ref[0, rr:rr + 1, :] == 1
        s = jnp.where(valid, scores[rr], NEG)
        m_old = m_s[rr]
        m_new = jnp.maximum(m_old, s)
        f = jnp.exp(m_old - m_new)
        p = jnp.where(valid, jnp.exp(s - m_new), 0.0)
        m_s[rr] = m_new
        l_s[rr] = l_s[rr] * f + p
        c = coarse[coarse_ch * rr:coarse_ch * (rr + 1)].reshape(-1, heads, half).astype(F32)
        a_s[rr] = a_s[rr] * f[None] + p[None] * c
        c = fines[rr].reshape(-1, heads, half).astype(F32)
        k_s[rr] = k_s[rr] * f[None] + p[None] * c

    @pl.when(t == pl.num_programs(0) - 1)
    def _():
        for rr in range(2):
            total = l_s[rr]
            lse = m_s[rr] + jnp.log(jnp.maximum(total, 0.5))
            ml_ref[heads * rr:heads * (rr + 1), :] = jnp.where(total > 0.0, lse, NEG)
            inv = (1.0 / jnp.maximum(total, 0.5))[None]
            a = (a_s[rr] * inv).reshape(coarse_ch, half)
            out_ref[coarse_ch * rr:coarse_ch * (rr + 1), :] = a.astype(BF)
            base = 2 * coarse_ch + 4 * fine_ch * rr
            k = (k_s[rr] * inv).reshape(4 * fine_ch, half)
            out_ref[base:base + 4 * fine_ch, :] = k.astype(BF)


def combine_kernel(heads, fine_ch, coarse_ch, ml_ref, ab_ref, wo_ref, wu_ref, out_ref):
    dates = ml_ref.shape[0]
    width = ml_ref.shape[2]
    for rr in range(2):
        ms = [ml_ref[d, heads * rr:heads * (rr + 1), :] for d in range(dates)]
        top = functools.reduce(jnp.maximum, ms)
        ws = [jnp.exp(m - top) for m in ms]
        inv = 1.0 / functools.reduce(jnp.add, ws)
        ws = [(w * inv)[None] for w in ws]

        def mix(base, size):
            parts = [
                ws[d] * ab_ref[d, base:base + size, :].reshape(-1, heads, width).astype(F32) for d in range(dates)
            ]
            return functools.reduce(jnp.add, parts).reshape(size, width).astype(BF)

        agg = mix(coarse_ch * rr, coarse_ch)
        skip = mix(2 * coarse_ch + 4 * fine_ch * rr, 4 * fine_ch)
        co = act(dot(wo_ref[...], agg)[None])[0].astype(BF)
        up = dot(wu_ref[...], co).astype(BF)
        n = 2 * fine_ch
        for a in range(2):
            base = 2 * n * (2 * rr + a)
            out_ref[base:base + n, :] = up[n * a:n * (a + 1)]
            out_ref[base + n:base + 2 * n, :] = skip[n * a:n * (a + 1)]


def decode_kernel(fine_ch, off_ref, top_ref, mid_ref, low_ref, wdec_ref, cls_ref, bias_ref, out_ref, s3):
    width = s3.shape[1]
    n = 4 * fine_ch
    rows = mid_ref.shape[0] // n
    for k in range(rows + 2):
        if k == 0:
            x = top_ref[...]
        elif k == rows + 1:
            x = low_ref[...]
        else:
            x = mid_ref[n * (k - 1):n * k, :]
        base = 2 * n * k
        s3[base:base + n, :] = x
        x = x.astype(F32).reshape(2, 2, fine_ch, width)
        half = 2 * fine_ch
        s3[base + n:base + n + half, :] = from_left(x[:, 1].reshape(half, width)).astype(BF)
        s3[base + n + half:base + 2 * n, :] = from_right(x[:, 0].reshape(half, width)).astype(BF)
    share = out_ref.shape[2]
    src = lax.broadcasted_iota(jnp.int32, (2 * width, share), 0)
    dst = lax.broadcasted_iota(jnp.int32, (2 * width, share), 1)
    pick = (src == off_ref[0] + lax.shift_right_logical(dst, 1) + (dst & 1) * width).astype(F32).astype(BF)
    for g in range(rows // 2):
        y = dot(wdec_ref[...], s3[4 * n * g:4 * n * g + 8 * n, :])
        y = act(y.reshape(4, fine_ch, width)).astype(BF)
        for ro in range(2):
            d = jnp.concatenate([y[2 * ro], y[2 * ro + 1]], axis=1)
            d = dot(d, pick).astype(BF)
            out_ref[:, 2 * g + ro, :] = dot(cls_ref[...], d) + bias_ref[...]


VMEM = pl.BlockSpec(memory_space=pltpu.VMEM)
SMEM = pl.BlockSpec(memory_space=pltpu.SMEM)


def neighbour_shift(x, step):
    count = lax.axis_size(ROWS)
    if step > 0:
        pairs = [(i, i + 1) for i in range(count - 1)]
    else:
        pairs = [(i + 1, i) for i in range(count - 1)]
    return lax.ppermute(x, ROWS, pairs)


def body(images, clouds, day_of_year, conv_first, conv_second, conv_down, conv_coarse, key_weight, query_weight,
         out_weight, up_weight, dec_weight, cls_weight, cls_bias):
    dates, bands, rows, cols = images.shape
    half = cols // 2
    fine_ch = conv_second.shape[1]
    coarse_ch = conv_coarse.shape[1]
    heads, key_size = query_weight.shape
    classes = cls_weight.shape[0]
    groups = lax.axis_size("date")
    me = lax.axis_index("date")
    band = lax.axis_index(ROWS)
    count = lax.axis_size(ROWS)

    flat = images.reshape(dates, bands * rows, cols)
    above = neighbour_shift(flat, 1)
    below = neighbour_shift(flat, -1)
    order = np.zeros((12 * 16, 3 * bands * rows), np.float32)
    for k in range(3):
        for r in range(rows):
            for c in range(bands):
                order[(rows * k + r) * 16 + c, (bands * k + c) * rows + r] = 1
    order = jnp.asarray(order, BF)

    edges = jnp.stack([(band > 0).astype(F32), (band < count - 1).astype(F32)])

    sel = np.zeros((256, 256), np.float32)
    for i in range(128):
        sel[2 * i, i] = 1
        sel[2 * i + 1, 128 + i] = 1
    sel = jnp.asarray(sel, BF)

    nk = 2 * heads * key_size
    n = 4 * fine_ch
    shapes = [(n, 256), (n, 16 * fine_ch), (coarse_ch, n), (2 * coarse_ch, 12 * coarse_ch), (nk, 2 * coarse_ch),
              (coarse_ch, coarse_ch), (n, 8 * n)]
    w1, w2, wd, wc, kw2, wo, wdec = pl.pallas_call(
        weights_kernel,
        in_specs=[VMEM] * 10,
        out_specs=[VMEM] * 7,
        out_shape=[jax.ShapeDtypeStruct(shape, BF) for shape in shapes],
        compiler_params=pltpu.CompilerParams(vmem_limit_bytes=48 * 1024 * 1024),
        cost_estimate=pl.CostEstimate(flops=10**9, bytes_accessed=6 * 10**6, transcendentals=0),
    )(regroup_matrix(fine_ch, heads), regroup_matrix(coarse_ch, heads), conv_first, conv_second, conv_down,
      conv_coarse, key_weight, out_weight, dec_weight, regroup_matrix(heads * key_size, heads))

    half_ch = coarse_ch // 2
    freqs = jnp.power(1000.0, -2.0 * jnp.arange(half_ch, dtype=F32) / coarse_ch)
    angles = day_of_year.astype(F32)[:, None] * freqs[None, :]
    encoding = jnp.concatenate([jnp.sin(angles), jnp.cos(angles)], axis=1)
    kb = jnp.dot(encoding, key_weight.astype(F32).T, precision=lax.Precision.HIGHEST)
    kb = regroup(kb, 1, heads)
    kb = jnp.concatenate([kb, kb], axis=1)[:, :, None]
    qv = jnp.transpose(query_weight).reshape(-1)
    qv = jnp.concatenate([qv, qv])[:, None]

    total = 2 * coarse_ch + 8 * fine_ch
    const = lambda *shape: pl.BlockSpec(shape, lambda t: (0,) * len(shape))
    ml, ab = pl.pallas_call(
        functools.partial(encode_kernel, heads, fine_ch, coarse_ch),
        grid=(dates,),
        in_specs=[
            SMEM,
            *[pl.BlockSpec((1, bands * rows, cols), lambda t: (t, 0, 0))] * 3,
            pl.BlockSpec((1, 2, half), lambda t: (t, 0, 0)),
            const(*order.shape),
            const(256, 256),
            const(*w1.shape),
            const(*w2.shape),
            const(*wd.shape),
            const(*wc.shape),
            const(*kw2.shape),
            pl.BlockSpec((1, nk, 1), lambda t: (t, 0, 0)),
            const(nk, 1),
        ],
        out_specs=[const(2 * heads, half), const(total, half)],
        out_shape=[jax.ShapeDtypeStruct((2 * heads, half), F32), jax.ShapeDtypeStruct((total, half), BF)],
        scratch_shapes=[
            pltpu.VMEM((12 * 64, half), BF),
            pltpu.VMEM((40 * fine_ch, half), BF),
            pltpu.VMEM((12 * coarse_ch, half), BF),
            pltpu.VMEM((2, heads, half), F32),
            pltpu.VMEM((2, heads, half), F32),
            pltpu.VMEM((2, coarse_ch // heads, heads, half), F32),
            pltpu.VMEM((2, 4 * fine_ch // heads, heads, half), F32),
        ],
        compiler_params=pltpu.CompilerParams(vmem_limit_bytes=48 * 1024 * 1024),
    )(edges, above, flat, below, clouds, order, sel, w1, w2, wd, wc, kw2, kb, qv)

    per = half // groups
    spans = []
    for k in range(groups):
        lo = max(0, (k * per - 1) // 128)
        hi = min(half // 128 - 1, (k * per + per) // 128)
        spans.append((lo, hi))
    width = max(hi - lo + 1 for lo, hi in spans) * 128
    starts = jnp.asarray([min(lo * 128, half - width) for lo, hi in spans], jnp.int32)

    def window(x, k):
        return lax.dynamic_slice_in_dim(x, starts[k], width, 1)

    mls, abs_ = [window(ml, me)], [window(ab, me)]
    for step in range(1, groups):
        to = lax.rem(me + step, groups)
        pairs = [(i, (i + step) % groups) for i in range(groups)]
        mls.append(lax.ppermute(window(ml, to), "date", pairs))
        abs_.append(lax.ppermute(window(ab, to), "date", pairs))
    joined = pl.pallas_call(
        functools.partial(combine_kernel, heads, fine_ch, coarse_ch),
        in_specs=[VMEM] * 4,
        out_specs=VMEM,
        out_shape=jax.ShapeDtypeStruct((rows * 4 * fine_ch, width), BF),
        compiler_params=pltpu.CompilerParams(vmem_limit_bytes=48 * 1024 * 1024),
    )(jnp.stack(mls), jnp.stack(abs_), wo, up_weight.reshape(4 * fine_ch, coarse_ch))

    top = neighbour_shift(joined[-n:], 1)
    low = neighbour_shift(joined[:n], -1)
    offset = (me * per - starts[me]).astype(jnp.int32).reshape(1)
    return pl.pallas_call(
        functools.partial(decode_kernel, fine_ch),
        in_specs=[SMEM] + [VMEM] * 6,
        out_specs=VMEM,
        out_shape=jax.ShapeDtypeStruct((classes, rows, cols // groups), F32),
        scratch_shapes=[pltpu.VMEM(((rows + 2) * 2 * n, width), BF)],
        compiler_params=pltpu.CompilerParams(vmem_limit_bytes=48 * 1024 * 1024),
    )(offset, top, joined, low, wdec, cls_weight, cls_bias[:, None])


def solution(mesh):
    return jax.shard_map(
        body,
        mesh=mesh,
        in_specs=(
            P("date", None, ("grp", "tile", "row"), None),
            P("date", ("grp", "tile", "row"), None),
            P(("grp", "date")),
        ) + (P(),) * 11,
        out_specs=P(None, ("grp", "tile", "row"), "date"),
        check_vma=False,
    )
```

```python
import functools

import jax
import jax.numpy as jnp
import numpy as np
from jax import lax
from jax.experimental import pallas as pl
from jax.experimental.pallas import tpu as pltpu
from jax.sharding import PartitionSpec as P

BF = jnp.bfloat16
F32 = jnp.float32
NEG = -1e30
ROWS = ("tile", "row")


def dot(a, b):
    return lax.dot_general(a, b, (((1,), (0,)), ((), ())), preferred_element_type=F32)


def act(y):
    ms = jnp.mean(y * y, axis=1, keepdims=True)
    return jnp.maximum(y * lax.rsqrt(ms + 1e-5), 0.0)


def from_left(x):
    lane = lax.broadcasted_iota(jnp.int32, x.shape, x.ndim - 1)
    return jnp.where(lane == 0, 0.0, pltpu.roll(x, 1, x.ndim - 1))


def from_right(x):
    n = x.shape[-1]
    lane = lax.broadcasted_iota(jnp.int32, x.shape, x.ndim - 1)
    return jnp.where(lane == n - 1, 0.0, pltpu.roll(x, n - 1, x.ndim - 1))


COL = ((1, 2, 0, None), (0, 1, None, 2))


def paired(tap, order):
    lines = []
    for ro in range(2):
        for po in range(2):
            line = []
            for ri in range(4):
                a = ri - ro
                for v, lo, hi in order:
                    b = COL[po][v]
                    if b is None or not 0 <= a < 3:
                        line.append(jnp.zeros((tap[0].shape[0], hi - lo), tap[0].dtype))
                    else:
                        line.append(tap[3 * a + b][:, lo:hi])
            lines.append(jnp.concatenate(line, axis=1))
    return lines


def weights_kernel(heads, first_ref, second_ref, down_ref, coarse_ref, key_ref, out_ref, dec_ref, w1_ref, w2_ref, wd_ref, wc_ref, kw_ref, wo_ref, wdec_ref):
    fine_ch = second_ref.shape[1]
    coarse_ch = coarse_ref.shape[1]
    bands = first_ref.shape[2]
    perm_f, perm_c = regroup_matrix(fine_ch, heads), regroup_matrix(coarse_ch, heads)
    perm_k = regroup_matrix(key_ref.shape[0], heads)

    def right(w, perm):
        return lax.dot_general(w, perm, (((1,), (1,)), ((), ())), preferred_element_type=F32)

    row = lax.broadcasted_iota(jnp.int32, (bands, 256), 0)
    col = lax.broadcasted_iota(jnp.int32, (bands, 256), 1)
    for ro in range(2):
        for po in range(2):
            total = jnp.zeros((fine_ch, 256), F32)
            for ri in range(4):
                for v in range(4):
                    a, b = ri - ro, COL[po][v]
                    if b is not None and 0 <= a < 3:
                        place = (col == row + (4 * ri + v) * 16).astype(F32).astype(BF)
                        total = total + dot(first_ref[3 * a + b], place)
            base = fine_ch * (2 * ro + po)
            w1_ref[base:base + fine_ch, :] = total.astype(BF)
    taps = [dot(perm_f, second_ref[k]) for k in range(9)]
    for k, line in enumerate(paired(taps, [(v, 0, fine_ch) for v in range(4)])):
        w2_ref[fine_ch * k:fine_ch * (k + 1), :] = line.astype(BF)
    wd_ref[...] = jnp.concatenate([right(down_ref[k], perm_f) for k in range(4)], axis=1).astype(BF)
    taps = [dot(perm_c, coarse_ref[k]).astype(BF) for k in range(9)]
    for ro in range(2):
        for ri in range(4):
            for v, b in enumerate((1, 0, 2)):
                a = ri - ro
                x = taps[3 * a + b] if 0 <= a < 3 else jnp.zeros((coarse_ch, coarse_ch), BF)
                base = coarse_ch * (3 * ri + v)
                wc_ref[coarse_ch * ro:coarse_ch * (ro + 1), base:base + coarse_ch] = x
    kw = right(dot(perm_k, key_ref[...]).astype(BF), perm_c).astype(BF)
    nk = kw.shape[0]
    kw_ref[...] = jnp.zeros(kw_ref.shape, BF)
    kw_ref[:nk, :coarse_ch] = kw
    kw_ref[nk:, coarse_ch:] = kw
    wo_ref[...] = right(out_ref[...], perm_c).astype(BF)
    taps = []
    for k in range(9):
        w = dec_ref[k]
        taps.append(jnp.concatenate([w[:, :fine_ch].astype(F32), right(w[:, fine_ch:], perm_f)], axis=1))
    up, skip = (0, fine_ch), (fine_ch, 2 * fine_ch)
    order = [(0, *up), (1, *up), (0, *skip), (1, *skip), (2, *up), (2, *skip), (3, *up), (3, *skip)]
    for k, line in enumerate(paired(taps, order)):
        wdec_ref[fine_ch * k:fine_ch * (k + 1), :] = line.astype(BF)


def regroup_matrix(n, heads):
    row = lax.broadcasted_iota(jnp.int32, (n, n), 0)
    col = lax.broadcasted_iota(jnp.int32, (n, n), 1)
    want = lax.rem(row, heads) * (n // heads) + lax.div(row, heads)
    return (col == want).astype(F32).astype(BF)


def regroup(w, axis, heads):
    axis = axis % w.ndim
    n = w.shape[axis] // heads
    shape = w.shape[:axis] + (heads, n) + w.shape[axis + 1:]
    return jnp.swapaxes(w.reshape(shape), axis, axis + 1).reshape(w.shape)


def encode_kernel(heads, fine_ch, coarse_ch, edge_ref, up_ref, img_ref, dn_ref, cloud_ref, order_ref, sel_ref, w1_ref, w2_ref, wd_ref, wc_ref,
                  kw_ref, kb_ref, q_ref, ml_ref, out_ref, xi, s1, s2, m_s, l_s, a_s, k_s):
    t = pl.program_id(0)
    half = xi.shape[1]
    bands = 16
    top, bottom = edge_ref[0], edge_ref[1]

    @pl.when(t == 0)
    def _():
        m_s[...] = jnp.full(m_s.shape, NEG, F32)
        l_s[...] = jnp.zeros(l_s.shape, F32)
        a_s[...] = jnp.zeros(a_s.shape, F32)
        k_s[...] = jnp.zeros(k_s.shape, F32)

    sel = sel_ref[...]
    img = jnp.concatenate([r[0].astype(F32) for r in (up_ref, img_ref, dn_ref)], axis=0).astype(BF)
    img = dot(order_ref[...], img).astype(BF)
    es, os = [], []
    for q in range(2 * half // 256):
        y = dot(img[:, 256 * q:256 * q + 256], sel)
        es.append(y[:, :128])
        os.append(y[:, 128:])
    e = jnp.concatenate(es, axis=1)
    o = jnp.concatenate(os, axis=1)
    variants = (e, o, from_left(o), from_right(e))
    for v, x in enumerate(variants):
        x = x.astype(BF)
        for r in range(12):
            xi[64 * r + bands * v:64 * r + bands * v + bands, :] = x[bands * r:bands * r + bands]
    for g in range(5):
        y = dot(w1_ref[...], xi[128 * g:128 * g + 256, :])
        y = act(y.reshape(4, fine_ch, half))
        for ro in range(2):
            k = 2 * g + ro
            e, o = y[2 * ro], y[2 * ro + 1]
            if k < 3:
                e, o = e * top, o * top
            if k > 6:
                e, o = e * bottom, o * bottom
            base = 4 * fine_ch * k
            for v, x in enumerate((e, o, from_left(o), from_right(e))):
                s1[base + fine_ch * v:base + fine_ch * (v + 1), :] = x.astype(BF)
    fines = []
    for g in range(4):
        y = dot(w2_ref[...], s1[8 * fine_ch * g:8 * fine_ch * g + 16 * fine_ch, :])
        f = act(y.reshape(4, fine_ch, half)).reshape(4 * fine_ch, half).astype(BF)
        if g in (1, 2):
            fines.append(f)
        low = act(dot(wd_ref[...], f)[None])[0]
        if g == 0:
            low = low * top
        if g == 3:
            low = low * bottom
        base = 3 * coarse_ch * g
        for v, x in enumerate((low, from_left(low), from_right(low))):
            s2[base + coarse_ch * v:base + coarse_ch * (v + 1), :] = x.astype(BF)
    y = dot(wc_ref[...], s2[...])
    coarse = act(y.reshape(2, coarse_ch, half)).reshape(2 * coarse_ch, half).astype(BF)
    km = (dot(kw_ref[...], coarse) + kb_ref[0]) * q_ref[...]
    km = km.reshape(2, km.shape[0] // (2 * heads), heads, half)
    scores = 0.5 * jnp.sum(km, axis=1)
    for rr in range(2):
        valid = cloud_ref[0, rr:rr + 1, :] == 1
        s = jnp.where(valid, scores[rr], NEG)
        m_old = m_s[rr]
        m_new = jnp.maximum(m_old, s)
        f = jnp.exp(m_old - m_new)
        p = jnp.where(valid, jnp.exp(s - m_new), 0.0)
        m_s[rr] = m_new
        l_s[rr] = l_s[rr] * f + p
        c = coarse[coarse_ch * rr:coarse_ch * (rr + 1)].reshape(-1, heads, half).astype(F32)
        a_s[rr] = a_s[rr] * f[None] + p[None] * c
        c = fines[rr].reshape(-1, heads, half).astype(F32)
        k_s[rr] = k_s[rr] * f[None] + p[None] * c

    @pl.when(t == pl.num_programs(0) - 1)
    def _():
        for rr in range(2):
            total = l_s[rr]
            lse = m_s[rr] + jnp.log(jnp.maximum(total, 0.5))
            ml_ref[heads * rr:heads * (rr + 1), :] = jnp.where(total > 0.0, lse, NEG)
            inv = (1.0 / jnp.maximum(total, 0.5))[None]
            a = (a_s[rr] * inv).reshape(coarse_ch, half)
            out_ref[coarse_ch * rr:coarse_ch * (rr + 1), :] = a.astype(BF)
            base = 2 * coarse_ch + 4 * fine_ch * rr
            k = (k_s[rr] * inv).reshape(4 * fine_ch, half)
            out_ref[base:base + 4 * fine_ch, :] = k.astype(BF)


def tail_kernel(heads, fine_ch, coarse_ch, groups, count, starts, per, ml_ref, ab_ref, wo_ref, wu_ref, wdec_ref,
                cls_ref, bias_ref, out_ref, ml_in, ab_in, edge_out, edge_in, s3, send, recv, edge_send, edge_recv):
    width = ab_in.shape[2]
    n = 4 * fine_ch
    rows = out_ref.shape[1]
    me = lax.axis_index("date")
    sides = lax.axis_size("row")
    band = lax.axis_index("tile") * sides + lax.axis_index("row")
    mesh_id = pl.DeviceIdType.MESH

    def start_of(k):
        at = starts[0]
        for j in range(1, groups):
            at = at + (starts[j] - starts[j - 1]) * ((k + groups - j) // groups)
        return pl.multiple_of(at, 128)

    def beside(step):
        other = band + step
        return {"tile": other // sides, "row": other % sides}

    barrier = pltpu.get_barrier_semaphore()
    for step in range(1, groups):
        pl.semaphore_signal(barrier, inc=1, device_id={"date": (me + step) % groups}, device_id_type=mesh_id)

    @pl.when(band > 0)
    def _():
        pl.semaphore_signal(barrier, inc=1, device_id=beside(-1), device_id_type=mesh_id)

    @pl.when(band < count - 1)
    def _():
        pl.semaphore_signal(barrier, inc=1, device_id=beside(1), device_id_type=mesh_id)

    pl.semaphore_wait(barrier, groups - 1 + (band + count - 1) // count + (2 * count - 2 - band) // count)

    copies = []
    for step in range(1, groups):
        to = (me + step) % groups
        cols = pl.ds(start_of(to), width)
        for kind, (src, dst) in enumerate(((ml_ref, ml_in), (ab_ref, ab_in))):
            at = 2 * (step - 1) + kind
            copies.append(pltpu.make_async_remote_copy(
                src_ref=src.at[:, cols], dst_ref=dst.at[step - 1], send_sem=send.at[at], recv_sem=recv.at[at],
                device_id={"date": to}, device_id_type=mesh_id))
            copies[-1].start()
    mine = start_of(me)
    cols = pl.ds(mine, width)
    src = lax.broadcasted_iota(jnp.int32, (2 * width, out_ref.shape[2]), 0)
    dst = lax.broadcasted_iota(jnp.int32, (2 * width, out_ref.shape[2]), 1)
    pick = src == me * per - mine + lax.shift_right_logical(dst, 1) + (dst & 1) * width
    pick = pick.astype(F32).astype(BF)
    for copy in copies:
        copy.wait()

    def put(k, x):
        base = 2 * n * k
        half = 2 * fine_ch
        s3[base:base + n, :] = x
        x = x.astype(F32).reshape(2, 2, fine_ch, width)
        s3[base + n:base + n + half, :] = from_left(x[:, 1].reshape(half, width)).astype(BF)
        s3[base + n + half:base + 2 * n, :] = from_right(x[:, 0].reshape(half, width)).astype(BF)

    joined = []
    for rr in range(2):
        head = slice(heads * rr, heads * (rr + 1))
        ms = [ml_ref[head, cols]] + [ml_in[d, head, :] for d in range(groups - 1)]
        top = functools.reduce(jnp.maximum, ms)
        ws = [jnp.exp(m - top) for m in ms]
        inv = 1.0 / functools.reduce(jnp.add, ws)
        ws = [(w * inv)[None] for w in ws]

        def mix(base, size):
            parts = [ab_ref[base:base + size, cols]] + [ab_in[d, base:base + size, :] for d in range(groups - 1)]
            parts = [w * x.reshape(-1, heads, width).astype(F32) for w, x in zip(ws, parts)]
            return functools.reduce(jnp.add, parts).reshape(size, width).astype(BF)

        agg = mix(coarse_ch * rr, coarse_ch)
        skip = mix(2 * coarse_ch + n * rr, n)
        co = act(dot(wo_ref[...], agg)[None])[0].astype(BF)
        up = dot(wu_ref[...], co).astype(BF)
        half = 2 * fine_ch
        for a in range(2):
            joined.append(jnp.concatenate([up[half * a:half * (a + 1)], skip[half * a:half * (a + 1)]], axis=0))
    edge_out[0] = joined[0]
    edge_out[1] = joined[rows - 1]
    above = pltpu.make_async_remote_copy(
        src_ref=edge_out.at[0], dst_ref=edge_in.at[1], send_sem=edge_send.at[0], recv_sem=edge_recv.at[1],
        device_id=beside(-1), device_id_type=mesh_id)
    below = pltpu.make_async_remote_copy(
        src_ref=edge_out.at[1], dst_ref=edge_in.at[0], send_sem=edge_send.at[1], recv_sem=edge_recv.at[0],
        device_id=beside(1), device_id_type=mesh_id)

    @pl.when(band > 0)
    def _():
        above.start()

    @pl.when(band < count - 1)
    def _():
        below.start()

    for k, x in enumerate(joined):
        put(k + 1, x)

    @pl.when(band > 0)
    def _():
        above.wait_send()
        below.wait_recv()

    @pl.when(band == 0)
    def _():
        edge_in[0] = jnp.zeros((n, width), BF)

    @pl.when(band < count - 1)
    def _():
        below.wait_send()
        above.wait_recv()

    @pl.when(band == count - 1)
    def _():
        edge_in[1] = jnp.zeros((n, width), BF)

    put(0, edge_in[0])
    put(rows + 1, edge_in[1])
    for g in range(rows // 2):
        y = dot(wdec_ref[...], s3[4 * n * g:4 * n * g + 8 * n, :])
        y = act(y.reshape(4, fine_ch, width)).astype(BF)
        for ro in range(2):
            d = jnp.concatenate([y[2 * ro], y[2 * ro + 1]], axis=1)
            d = dot(d, pick).astype(BF)
            out_ref[:, 2 * g + ro, :] = dot(cls_ref[...], d) + bias_ref[...]


VMEM = pl.BlockSpec(memory_space=pltpu.VMEM)
SMEM = pl.BlockSpec(memory_space=pltpu.SMEM)


def neighbour_shift(x, step):
    count = lax.axis_size(ROWS)
    if step > 0:
        pairs = [(i, i + 1) for i in range(count - 1)]
    else:
        pairs = [(i + 1, i) for i in range(count - 1)]
    return lax.ppermute(x, ROWS, pairs)


def body(images, clouds, day_of_year, conv_first, conv_second, conv_down, conv_coarse, key_weight, query_weight,
         out_weight, up_weight, dec_weight, cls_weight, cls_bias):
    dates, bands, rows, cols = images.shape
    half = cols // 2
    fine_ch = conv_second.shape[1]
    coarse_ch = conv_coarse.shape[1]
    heads, key_size = query_weight.shape
    classes = cls_weight.shape[0]
    groups = lax.axis_size("date")
    band = lax.axis_index(ROWS)
    count = lax.axis_size(ROWS)

    flat = images.reshape(dates, bands * rows, cols)
    above = neighbour_shift(flat, 1)
    below = neighbour_shift(flat, -1)
    order = np.zeros((12 * 16, 3 * bands * rows), np.float32)
    for k in range(3):
        for r in range(rows):
            for c in range(bands):
                order[(rows * k + r) * 16 + c, (bands * k + c) * rows + r] = 1
    order = jnp.asarray(order, BF)

    edges = jnp.stack([(band > 0).astype(F32), (band < count - 1).astype(F32)])

    sel = np.zeros((256, 256), np.float32)
    for i in range(128):
        sel[2 * i, i] = 1
        sel[2 * i + 1, 128 + i] = 1
    sel = jnp.asarray(sel, BF)

    nk = 2 * heads * key_size
    n = 4 * fine_ch
    const = lambda *shape: pl.BlockSpec(shape, lambda t: (0,) * len(shape))
    raw = (conv_first, conv_second, conv_down, conv_coarse, key_weight, out_weight, dec_weight)
    shapes = [(n, 256), (n, 16 * fine_ch), (coarse_ch, n), (2 * coarse_ch, 12 * coarse_ch), (nk, 2 * coarse_ch),
              (coarse_ch, coarse_ch), (n, 8 * n)]
    w1, w2, wd, wc, kw2, wo, wdec = pl.pallas_call(
        functools.partial(weights_kernel, heads),
        grid=(1,),
        in_specs=[const(*w.shape) for w in raw],
        out_specs=[const(*shape) for shape in shapes],
        out_shape=[jax.ShapeDtypeStruct(shape, BF) for shape in shapes],
        compiler_params=pltpu.CompilerParams(vmem_limit_bytes=48 * 1024 * 1024),
        cost_estimate=pl.CostEstimate(flops=10**9, bytes_accessed=6 * 10**6, transcendentals=0),
    )(*raw)

    half_ch = coarse_ch // 2
    freqs = jnp.power(1000.0, -2.0 * jnp.arange(half_ch, dtype=F32) / coarse_ch)
    angles = day_of_year.astype(F32)[:, None] * freqs[None, :]
    encoding = jnp.concatenate([jnp.sin(angles), jnp.cos(angles)], axis=1)
    kb = jnp.dot(encoding, key_weight.astype(F32).T, precision=lax.Precision.HIGHEST)
    kb = regroup(kb, 1, heads)
    kb = jnp.concatenate([kb, kb], axis=1)[:, :, None]
    qv = jnp.transpose(query_weight).reshape(-1)
    qv = jnp.concatenate([qv, qv])[:, None]

    total = 2 * coarse_ch + 8 * fine_ch
    ml, ab = pl.pallas_call(
        functools.partial(encode_kernel, heads, fine_ch, coarse_ch),
        grid=(dates,),
        in_specs=[
            SMEM,
            *[pl.BlockSpec((1, bands * rows, cols), lambda t: (t, 0, 0))] * 3,
            pl.BlockSpec((1, 2, half), lambda t: (t, 0, 0)),
            const(*order.shape),
            const(256, 256),
            const(*w1.shape),
            const(*w2.shape),
            const(*wd.shape),
            const(*wc.shape),
            const(*kw2.shape),
            pl.BlockSpec((1, nk, 1), lambda t: (t, 0, 0)),
            const(nk, 1),
        ],
        out_specs=[const(2 * heads, half), const(total, half)],
        out_shape=[jax.ShapeDtypeStruct((2 * heads, half), F32), jax.ShapeDtypeStruct((total, half), BF)],
        scratch_shapes=[
            pltpu.VMEM((12 * 64, half), BF),
            pltpu.VMEM((40 * fine_ch, half), BF),
            pltpu.VMEM((12 * coarse_ch, half), BF),
            pltpu.VMEM((2, heads, half), F32),
            pltpu.VMEM((2, heads, half), F32),
            pltpu.VMEM((2, coarse_ch // heads, heads, half), F32),
            pltpu.VMEM((2, 4 * fine_ch // heads, heads, half), F32),
        ],
        compiler_params=pltpu.CompilerParams(vmem_limit_bytes=48 * 1024 * 1024),
    )(edges, above, flat, below, clouds, order, sel, w1, w2, wd, wc, kw2, kb, qv)

    per = half // groups
    spans = []
    for k in range(groups):
        lo = max(0, (k * per - 1) // 128)
        hi = min(half // 128 - 1, (k * per + per) // 128)
        spans.append((lo, hi))
    width = max(hi - lo + 1 for lo, hi in spans) * 128
    starts = [min(lo * 128, half - width) for lo, hi in spans]
    return pl.pallas_call(
        functools.partial(tail_kernel, heads, fine_ch, coarse_ch, groups, count, starts, per),
        in_specs=[VMEM] * 7,
        out_specs=VMEM,
        out_shape=jax.ShapeDtypeStruct((classes, rows, cols // groups), F32),
        scratch_shapes=[
            pltpu.VMEM((groups - 1, 2 * heads, width), F32),
            pltpu.VMEM((groups - 1, total, width), BF),
            pltpu.VMEM((2, n, width), BF),
            pltpu.VMEM((2, n, width), BF),
            pltpu.VMEM(((rows + 2) * 2 * n, width), BF),
            pltpu.SemaphoreType.DMA((2 * (groups - 1),)),
            pltpu.SemaphoreType.DMA((2 * (groups - 1),)),
            pltpu.SemaphoreType.DMA((2,)),
            pltpu.SemaphoreType.DMA((2,)),
        ],
        compiler_params=pltpu.CompilerParams(
            vmem_limit_bytes=48 * 1024 * 1024, collective_id=0, has_side_effects=True),
    )(ml, ab, wo, up_weight.reshape(n, coarse_ch), wdec, cls_weight, cls_bias[:, None])


def solution(mesh):
    return jax.shard_map(
        body,
        mesh=mesh,
        in_specs=(
            P("date", None, ("grp", "tile", "row"), None),
            P("date", ("grp", "tile", "row"), None),
            P(("grp", "date")),
        ) + (P(),) * 11,
        out_specs=P(None, ("grp", "tile", "row"), "date"),
        check_vma=False,
    )
```

```python
import functools

import jax
import jax.numpy as jnp
import numpy as np
from jax import lax
from jax.experimental import pallas as pl
from jax.experimental.pallas import tpu as pltpu
from jax.sharding import PartitionSpec as P

BF = jnp.bfloat16
F32 = jnp.float32
NEG = -1e30
ROWS = ("tile", "row")


def dot(a, b):
    return lax.dot_general(a, b, (((1,), (0,)), ((), ())), preferred_element_type=F32)


def act(y):
    ms = jnp.mean(y * y, axis=1, keepdims=True)
    return jnp.maximum(y * lax.rsqrt(ms + 1e-5), 0.0)


def from_left(x):
    lane = lax.broadcasted_iota(jnp.int32, x.shape, x.ndim - 1)
    return jnp.where(lane == 0, 0.0, pltpu.roll(x, 1, x.ndim - 1))


def from_right(x):
    n = x.shape[-1]
    lane = lax.broadcasted_iota(jnp.int32, x.shape, x.ndim - 1)
    return jnp.where(lane == n - 1, 0.0, pltpu.roll(x, n - 1, x.ndim - 1))


COL = ((1, 2, 0, None), (0, 1, None, 2))


def paired(tap, order):
    lines = []
    for ro in range(2):
        for po in range(2):
            line = []
            for ri in range(4):
                a = ri - ro
                for v, lo, hi in order:
                    b = COL[po][v]
                    if b is None or not 0 <= a < 3:
                        line.append(jnp.zeros((tap[0].shape[0], hi - lo), tap[0].dtype))
                    else:
                        line.append(tap[3 * a + b][:, lo:hi])
            lines.append(jnp.concatenate(line, axis=1))
    return lines


def weights_kernel(heads, first_ref, second_ref, down_ref, coarse_ref, key_ref, out_ref, dec_ref, w1_ref, w2_ref, wd_ref, wc_ref, kw_ref, wo_ref, wdec_ref):
    fine_ch = second_ref.shape[1]
    coarse_ch = coarse_ref.shape[1]
    bands = first_ref.shape[2]
    perm_f, perm_c = regroup_matrix(fine_ch, heads), regroup_matrix(coarse_ch, heads)
    perm_k = regroup_matrix(key_ref.shape[0], heads)

    def right(w, perm):
        return lax.dot_general(w, perm, (((1,), (1,)), ((), ())), preferred_element_type=F32)

    row = lax.broadcasted_iota(jnp.int32, (bands, 256), 0)
    col = lax.broadcasted_iota(jnp.int32, (bands, 256), 1)
    for ro in range(2):
        for po in range(2):
            total = jnp.zeros((fine_ch, 256), F32)
            for ri in range(4):
                for v in range(4):
                    a, b = ri - ro, COL[po][v]
                    if b is not None and 0 <= a < 3:
                        place = (col == row + (4 * ri + v) * 16).astype(F32).astype(BF)
                        total = total + dot(first_ref[3 * a + b], place)
            base = fine_ch * (2 * ro + po)
            w1_ref[base:base + fine_ch, :] = total.astype(BF)
    taps = [dot(perm_f, second_ref[k]) for k in range(9)]
    for k, line in enumerate(paired(taps, [(v, 0, fine_ch) for v in range(4)])):
        w2_ref[fine_ch * k:fine_ch * (k + 1), :] = line.astype(BF)
    wd_ref[...] = jnp.concatenate([right(down_ref[k], perm_f) for k in range(4)], axis=1).astype(BF)
    taps = [dot(perm_c, coarse_ref[k]).astype(BF) for k in range(9)]
    for ro in range(2):
        for ri in range(4):
            for v, b in enumerate((1, 0, 2)):
                a = ri - ro
                x = taps[3 * a + b] if 0 <= a < 3 else jnp.zeros((coarse_ch, coarse_ch), BF)
                base = coarse_ch * (3 * ri + v)
                wc_ref[coarse_ch * ro:coarse_ch * (ro + 1), base:base + coarse_ch] = x
    kw = right(dot(perm_k, key_ref[...]).astype(BF), perm_c).astype(BF)
    nk = kw.shape[0]
    kw_ref[...] = jnp.zeros(kw_ref.shape, BF)
    kw_ref[:nk, :coarse_ch] = kw
    kw_ref[nk:, coarse_ch:] = kw
    wo_ref[...] = right(out_ref[...], perm_c).astype(BF)
    taps = []
    for k in range(9):
        w = dec_ref[k]
        taps.append(jnp.concatenate([w[:, :fine_ch].astype(F32), right(w[:, fine_ch:], perm_f)], axis=1))
    up, skip = (0, fine_ch), (fine_ch, 2 * fine_ch)
    order = [(0, *up), (1, *up), (0, *skip), (1, *skip), (2, *up), (2, *skip), (3, *up), (3, *skip)]
    for k, line in enumerate(paired(taps, order)):
        wdec_ref[fine_ch * k:fine_ch * (k + 1), :] = line.astype(BF)


def regroup_matrix(n, heads):
    row = lax.broadcasted_iota(jnp.int32, (n, n), 0)
    col = lax.broadcasted_iota(jnp.int32, (n, n), 1)
    want = lax.rem(row, heads) * (n // heads) + lax.div(row, heads)
    return (col == want).astype(F32).astype(BF)


def regroup(w, axis, heads):
    axis = axis % w.ndim
    n = w.shape[axis] // heads
    shape = w.shape[:axis] + (heads, n) + w.shape[axis + 1:]
    return jnp.swapaxes(w.reshape(shape), axis, axis + 1).reshape(w.shape)


def encode_kernel(heads, fine_ch, coarse_ch, edge_ref, up_ref, img_ref, dn_ref, cloud_ref, order_ref, sel_ref, w1_ref, w2_ref, wd_ref, wc_ref,
                  kw_ref, kb_ref, q_ref, ml_ref, out_ref, xi, s1, s2, m_s, l_s, a_s, k_s):
    t = pl.program_id(0)
    half = xi.shape[1]
    bands = 16
    top, bottom = edge_ref[0], edge_ref[1]

    @pl.when(t == 0)
    def _():
        m_s[...] = jnp.full(m_s.shape, NEG, F32)
        l_s[...] = jnp.zeros(l_s.shape, F32)
        a_s[...] = jnp.zeros(a_s.shape, F32)
        k_s[...] = jnp.zeros(k_s.shape, F32)

    sel = sel_ref[...]
    img = jnp.concatenate([r[0].astype(F32) for r in (up_ref, img_ref, dn_ref)], axis=0).astype(BF)
    img = dot(order_ref[...], img).astype(BF)
    es, os = [], []
    for q in range(2 * half // 256):
        y = dot(img[:, 256 * q:256 * q + 256], sel)
        es.append(y[:, :128])
        os.append(y[:, 128:])
    e = jnp.concatenate(es, axis=1)
    o = jnp.concatenate(os, axis=1)
    variants = (e, o, from_left(o), from_right(e))
    for v, x in enumerate(variants):
        x = x.astype(BF)
        for r in range(12):
            xi[64 * r + bands * v:64 * r + bands * v + bands, :] = x[bands * r:bands * r + bands]
    for g in range(5):
        y = dot(w1_ref[...], xi[128 * g:128 * g + 256, :])
        y = act(y.reshape(4, fine_ch, half))
        for ro in range(2):
            k = 2 * g + ro
            e, o = y[2 * ro], y[2 * ro + 1]
            if k < 3:
                e, o = e * top, o * top
            if k > 6:
                e, o = e * bottom, o * bottom
            base = 4 * fine_ch * k
            for v, x in enumerate((e, o, from_left(o), from_right(e))):
                s1[base + fine_ch * v:base + fine_ch * (v + 1), :] = x.astype(BF)
    fines = []
    for g in range(4):
        y = dot(w2_ref[...], s1[8 * fine_ch * g:8 * fine_ch * g + 16 * fine_ch, :])
        f = act(y.reshape(4, fine_ch, half)).reshape(4 * fine_ch, half).astype(BF)
        if g in (1, 2):
            fines.append(f)
        low = act(dot(wd_ref[...], f)[None])[0]
        if g == 0:
            low = low * top
        if g == 3:
            low = low * bottom
        base = 3 * coarse_ch * g
        for v, x in enumerate((low, from_left(low), from_right(low))):
            s2[base + coarse_ch * v:base + coarse_ch * (v + 1), :] = x.astype(BF)
    y = dot(wc_ref[...], s2[...])
    coarse = act(y.reshape(2, coarse_ch, half)).reshape(2 * coarse_ch, half).astype(BF)
    km = (dot(kw_ref[...], coarse) + kb_ref[0]) * q_ref[...]
    km = km.reshape(2, km.shape[0] // (2 * heads), heads, half)
    scores = 0.5 * jnp.sum(km, axis=1)
    for rr in range(2):
        valid = cloud_ref[0, rr:rr + 1, :] == 1
        s = jnp.where(valid, scores[rr], NEG)
        m_old = m_s[rr]
        m_new = jnp.maximum(m_old, s)
        f = jnp.exp(m_old - m_new)
        p = jnp.where(valid, jnp.exp(s - m_new), 0.0)
        m_s[rr] = m_new
        l_s[rr] = l_s[rr] * f + p
        c = coarse[coarse_ch * rr:coarse_ch * (rr + 1)].reshape(-1, heads, half).astype(F32)
        a_s[rr] = a_s[rr] * f[None] + p[None] * c
        c = fines[rr].reshape(-1, heads, half).astype(F32)
        k_s[rr] = k_s[rr] * f[None] + p[None] * c

    @pl.when(t == pl.num_programs(0) - 1)
    def _():
        for rr in range(2):
            total = l_s[rr]
            lse = m_s[rr] + jnp.log(jnp.maximum(total, 0.5))
            ml_ref[heads * rr:heads * (rr + 1), :] = jnp.where(total > 0.0, lse, NEG)
            inv = (1.0 / jnp.maximum(total, 0.5))[None]
            a = (a_s[rr] * inv).reshape(coarse_ch, half)
            out_ref[coarse_ch * rr:coarse_ch * (rr + 1), :] = a.astype(BF)
            base = 2 * coarse_ch + 4 * fine_ch * rr
            k = (k_s[rr] * inv).reshape(4 * fine_ch, half)
            out_ref[base:base + 4 * fine_ch, :] = k.astype(BF)


def tail_kernel(heads, fine_ch, coarse_ch, groups, count, starts, per, ml_ref, ab_ref, wo_ref, wu_ref, wdec_ref,
                cls_ref, bias_ref, out_ref, ml_in, ab_in, halo_out, halo_in, edge_out, edge_in, s3, send, recv, edge_send, edge_recv):
    width = ab_in.shape[2]
    n = 4 * fine_ch
    rows = out_ref.shape[1]
    packed = groups == 2 and per % 128 == 0 and width == per + 128
    me = lax.axis_index("date")
    sides = lax.axis_size("row")
    band = lax.axis_index("tile") * sides + lax.axis_index("row")
    mesh_id = pl.DeviceIdType.MESH

    def start_of(k):
        at = starts[0]
        for j in range(1, groups):
            at = at + (starts[j] - starts[j - 1]) * ((k + groups - j) // groups)
        return pl.multiple_of(at, 128)

    def beside(step):
        other = band + step
        return {"tile": other // sides, "row": other % sides}

    barrier = pltpu.get_barrier_semaphore()
    for step in range(1, groups):
        pl.semaphore_signal(barrier, inc=1, device_id={"date": (me + step) % groups}, device_id_type=mesh_id)

    @pl.when(band > 0)
    def _():
        pl.semaphore_signal(barrier, inc=1, device_id=beside(-1), device_id_type=mesh_id)

    @pl.when(band < count - 1)
    def _():
        pl.semaphore_signal(barrier, inc=1, device_id=beside(1), device_id_type=mesh_id)

    pl.semaphore_wait(barrier, groups - 1 + (band + count - 1) // count + (2 * count - 2 - band) // count)

    copies = []
    for step in range(1, groups):
        to = (me + step) % groups
        cols = pl.ds(start_of(to), width)
        pairs = [(ml_ref.at[:, cols], ml_in.at[step - 1])]
        if packed:
            own = ab_ref.at[:, pl.ds(pl.multiple_of(per * to, 128), per)]
            pairs.append((own, ab_in.at[0, :, pl.ds(pl.multiple_of(128 * to, 128), per)]))
            block = ab_ref[:, pl.ds(pl.multiple_of(per - 128 + 128 * me, 128), 128)]
            lane = lax.broadcasted_iota(jnp.int32, (16, 128), 1)
            line = lax.broadcasted_iota(jnp.int32, (16, 128), 0)
            mark = ((line == 0) & (lane == 127 * (1 - me))).astype(F32).astype(BF)
            halo_out[...] = lax.dot_general(
                mark, block, (((1,), (1,)), ((), ())), preferred_element_type=F32).astype(BF)
            pairs.append((halo_out, halo_in))
        else:
            pairs.append((ab_ref.at[:, cols], ab_in.at[step - 1]))
        for kind, (src, dst) in enumerate(pairs):
            at = 3 * (step - 1) + kind
            copies.append(pltpu.make_async_remote_copy(
                src_ref=src, dst_ref=dst, send_sem=send.at[at], recv_sem=recv.at[at],
                device_id={"date": to}, device_id_type=mesh_id))
            copies[-1].start()
    mine = start_of(me)
    cols = pl.ds(mine, width)
    src = lax.broadcasted_iota(jnp.int32, (2 * width, out_ref.shape[2]), 0)
    dst = lax.broadcasted_iota(jnp.int32, (2 * width, out_ref.shape[2]), 1)
    pick = src == me * per - mine + lax.shift_right_logical(dst, 1) + (dst & 1) * width
    pick = pick.astype(F32).astype(BF)
    for copy in copies:
        copy.wait()
    if packed:
        lane = lax.broadcasted_iota(jnp.int32, (16, 128), 1)
        line = lax.broadcasted_iota(jnp.int32, (16, 128), 0)
        mark = ((line == 0) & (lane == 127 * me)).astype(F32).astype(BF)
        block = lax.dot_general(halo_in[...], mark, (((0,), (0,)), ((), ())), preferred_element_type=F32)
        ab_in[0, :, pl.ds(pl.multiple_of(per * (1 - me), 128), 128)] = block.astype(BF)

    def put(k, x):
        base = 2 * n * k
        half = 2 * fine_ch
        s3[base:base + n, :] = x
        x = x.astype(F32).reshape(2, 2, fine_ch, width)
        s3[base + n:base + n + half, :] = from_left(x[:, 1].reshape(half, width)).astype(BF)
        s3[base + n + half:base + 2 * n, :] = from_right(x[:, 0].reshape(half, width)).astype(BF)

    joined = []
    for rr in range(2):
        head = slice(heads * rr, heads * (rr + 1))
        ms = [ml_ref[head, cols]] + [ml_in[d, head, :] for d in range(groups - 1)]
        top = functools.reduce(jnp.maximum, ms)
        ws = [jnp.exp(m - top) for m in ms]
        inv = 1.0 / functools.reduce(jnp.add, ws)
        ws = [(w * inv)[None] for w in ws]

        def mix(base, size):
            parts = [ab_ref[base:base + size, cols]] + [ab_in[d, base:base + size, :] for d in range(groups - 1)]
            parts = [w * x.reshape(-1, heads, width).astype(F32) for w, x in zip(ws, parts)]
            return functools.reduce(jnp.add, parts).reshape(size, width).astype(BF)

        agg = mix(coarse_ch * rr, coarse_ch)
        skip = mix(2 * coarse_ch + n * rr, n)
        co = act(dot(wo_ref[...], agg)[None])[0].astype(BF)
        up = dot(wu_ref[...], co).astype(BF)
        half = 2 * fine_ch
        for a in range(2):
            joined.append(jnp.concatenate([up[half * a:half * (a + 1)], skip[half * a:half * (a + 1)]], axis=0))
    edge_out[0] = joined[0]
    edge_out[1] = joined[rows - 1]
    above = pltpu.make_async_remote_copy(
        src_ref=edge_out.at[0], dst_ref=edge_in.at[1], send_sem=edge_send.at[0], recv_sem=edge_recv.at[1],
        device_id=beside(-1), device_id_type=mesh_id)
    below = pltpu.make_async_remote_copy(
        src_ref=edge_out.at[1], dst_ref=edge_in.at[0], send_sem=edge_send.at[1], recv_sem=edge_recv.at[0],
        device_id=beside(1), device_id_type=mesh_id)

    @pl.when(band > 0)
    def _():
        above.start()

    @pl.when(band < count - 1)
    def _():
        below.start()

    for k, x in enumerate(joined):
        put(k + 1, x)

    @pl.when(band > 0)
    def _():
        above.wait_send()
        below.wait_recv()

    @pl.when(band == 0)
    def _():
        edge_in[0] = jnp.zeros((n, width), BF)

    @pl.when(band < count - 1)
    def _():
        below.wait_send()
        above.wait_recv()

    @pl.when(band == count - 1)
    def _():
        edge_in[1] = jnp.zeros((n, width), BF)

    put(0, edge_in[0])
    put(rows + 1, edge_in[1])
    for g in range(rows // 2):
        y = dot(wdec_ref[...], s3[4 * n * g:4 * n * g + 8 * n, :])
        y = act(y.reshape(4, fine_ch, width)).astype(BF)
        for ro in range(2):
            d = jnp.concatenate([y[2 * ro], y[2 * ro + 1]], axis=1)
            d = dot(d, pick).astype(BF)
            out_ref[:, 2 * g + ro, :] = dot(cls_ref[...], d) + bias_ref[...]


VMEM = pl.BlockSpec(memory_space=pltpu.VMEM)
SMEM = pl.BlockSpec(memory_space=pltpu.SMEM)


def neighbour_shift(x, step):
    count = lax.axis_size(ROWS)
    if step > 0:
        pairs = [(i, i + 1) for i in range(count - 1)]
    else:
        pairs = [(i + 1, i) for i in range(count - 1)]
    return lax.ppermute(x, ROWS, pairs)


def body(images, clouds, day_of_year, conv_first, conv_second, conv_down, conv_coarse, key_weight, query_weight,
         out_weight, up_weight, dec_weight, cls_weight, cls_bias):
    dates, bands, rows, cols = images.shape
    half = cols // 2
    fine_ch = conv_second.shape[1]
    coarse_ch = conv_coarse.shape[1]
    heads, key_size = query_weight.shape
    classes = cls_weight.shape[0]
    groups = lax.axis_size("date")
    band = lax.axis_index(ROWS)
    count = lax.axis_size(ROWS)

    flat = images.reshape(dates, bands * rows, cols)
    above = neighbour_shift(flat, 1)
    below = neighbour_shift(flat, -1)
    order = np.zeros((12 * 16, 3 * bands * rows), np.float32)
    for k in range(3):
        for r in range(rows):
            for c in range(bands):
                order[(rows * k + r) * 16 + c, (bands * k + c) * rows + r] = 1
    order = jnp.asarray(order, BF)

    edges = jnp.stack([(band > 0).astype(F32), (band < count - 1).astype(F32)])

    sel = np.zeros((256, 256), np.float32)
    for i in range(128):
        sel[2 * i, i] = 1
        sel[2 * i + 1, 128 + i] = 1
    sel = jnp.asarray(sel, BF)

    nk = 2 * heads * key_size
    n = 4 * fine_ch
    const = lambda *shape: pl.BlockSpec(shape, lambda t: (0,) * len(shape))
    raw = (conv_first, conv_second, conv_down, conv_coarse, key_weight, out_weight, dec_weight)
    shapes = [(n, 256), (n, 16 * fine_ch), (coarse_ch, n), (2 * coarse_ch, 12 * coarse_ch), (nk, 2 * coarse_ch),
              (coarse_ch, coarse_ch), (n, 8 * n)]
    w1, w2, wd, wc, kw2, wo, wdec = pl.pallas_call(
        functools.partial(weights_kernel, heads),
        grid=(1,),
        in_specs=[const(*w.shape) for w in raw],
        out_specs=[const(*shape) for shape in shapes],
        out_shape=[jax.ShapeDtypeStruct(shape, BF) for shape in shapes],
        compiler_params=pltpu.CompilerParams(vmem_limit_bytes=48 * 1024 * 1024),
        cost_estimate=pl.CostEstimate(flops=10**9, bytes_accessed=6 * 10**6, transcendentals=0),
    )(*raw)

    half_ch = coarse_ch // 2
    freqs = jnp.power(1000.0, -2.0 * jnp.arange(half_ch, dtype=F32) / coarse_ch)
    angles = day_of_year.astype(F32)[:, None] * freqs[None, :]
    encoding = jnp.concatenate([jnp.sin(angles), jnp.cos(angles)], axis=1)
    kb = jnp.dot(encoding, key_weight.astype(F32).T, precision=lax.Precision.HIGHEST)
    kb = regroup(kb, 1, heads)
    kb = jnp.concatenate([kb, kb], axis=1)[:, :, None]
    qv = jnp.transpose(query_weight).reshape(-1)
    qv = jnp.concatenate([qv, qv])[:, None]

    total = 2 * coarse_ch + 8 * fine_ch
    ml, ab = pl.pallas_call(
        functools.partial(encode_kernel, heads, fine_ch, coarse_ch),
        grid=(dates,),
        in_specs=[
            SMEM,
            *[pl.BlockSpec((1, bands * rows, cols), lambda t: (t, 0, 0))] * 3,
            pl.BlockSpec((1, 2, half), lambda t: (t, 0, 0)),
            const(*order.shape),
            const(256, 256),
            const(*w1.shape),
            const(*w2.shape),
            const(*wd.shape),
            const(*wc.shape),
            const(*kw2.shape),
            pl.BlockSpec((1, nk, 1), lambda t: (t, 0, 0)),
            const(nk, 1),
        ],
        out_specs=[const(2 * heads, half), const(total, half)],
        out_shape=[jax.ShapeDtypeStruct((2 * heads, half), F32), jax.ShapeDtypeStruct((total, half), BF)],
        scratch_shapes=[
            pltpu.VMEM((12 * 64, half), BF),
            pltpu.VMEM((40 * fine_ch, half), BF),
            pltpu.VMEM((12 * coarse_ch, half), BF),
            pltpu.VMEM((2, heads, half), F32),
            pltpu.VMEM((2, heads, half), F32),
            pltpu.VMEM((2, coarse_ch // heads, heads, half), F32),
            pltpu.VMEM((2, 4 * fine_ch // heads, heads, half), F32),
        ],
        compiler_params=pltpu.CompilerParams(vmem_limit_bytes=48 * 1024 * 1024),
    )(edges, above, flat, below, clouds, order, sel, w1, w2, wd, wc, kw2, kb, qv)

    per = half // groups
    spans = []
    for k in range(groups):
        lo = max(0, (k * per - 1) // 128)
        hi = min(half // 128 - 1, (k * per + per) // 128)
        spans.append((lo, hi))
    width = max(hi - lo + 1 for lo, hi in spans) * 128
    starts = [min(lo * 128, half - width) for lo, hi in spans]
    return pl.pallas_call(
        functools.partial(tail_kernel, heads, fine_ch, coarse_ch, groups, count, starts, per),
        in_specs=[VMEM] * 7,
        out_specs=VMEM,
        out_shape=jax.ShapeDtypeStruct((classes, rows, cols // groups), F32),
        scratch_shapes=[
            pltpu.VMEM((groups - 1, 2 * heads, width), F32),
            pltpu.VMEM((groups - 1, total, width), BF),
            pltpu.VMEM((16, total), BF),
            pltpu.VMEM((16, total), BF),
            pltpu.VMEM((2, n, width), BF),
            pltpu.VMEM((2, n, width), BF),
            pltpu.VMEM(((rows + 2) * 2 * n, width), BF),
            pltpu.SemaphoreType.DMA((3 * (groups - 1),)),
            pltpu.SemaphoreType.DMA((3 * (groups - 1),)),
            pltpu.SemaphoreType.DMA((2,)),
            pltpu.SemaphoreType.DMA((2,)),
        ],
        compiler_params=pltpu.CompilerParams(
            vmem_limit_bytes=48 * 1024 * 1024, collective_id=0, has_side_effects=True),
    )(ml, ab, wo, up_weight.reshape(n, coarse_ch), wdec, cls_weight, cls_bias[:, None])


def solution(mesh):
    return jax.shard_map(
        body,
        mesh=mesh,
        in_specs=(
            P("date", None, ("grp", "tile", "row"), None),
            P("date", ("grp", "tile", "row"), None),
            P(("grp", "date")),
        ) + (P(),) * 11,
        out_specs=P(None, ("grp", "tile", "row"), "date"),
        check_vma=False,
    )
```

```python
import functools

import jax
import jax.numpy as jnp
import numpy as np
from jax import lax
from jax.experimental import pallas as pl
from jax.experimental.pallas import tpu as pltpu
from jax.sharding import PartitionSpec as P

BF = jnp.bfloat16
F32 = jnp.float32
NEG = -1e30
ROWS = ("tile", "row")


def dot(a, b):
    return lax.dot_general(a, b, (((1,), (0,)), ((), ())), preferred_element_type=F32)


def act(y):
    ms = jnp.mean(y * y, axis=1, keepdims=True)
    return jnp.maximum(y * lax.rsqrt(ms + 1e-5), 0.0)


def from_left(x):
    lane = lax.broadcasted_iota(jnp.int32, x.shape, x.ndim - 1)
    return jnp.where(lane == 0, 0.0, pltpu.roll(x, 1, x.ndim - 1))


def from_right(x):
    n = x.shape[-1]
    lane = lax.broadcasted_iota(jnp.int32, x.shape, x.ndim - 1)
    return jnp.where(lane == n - 1, 0.0, pltpu.roll(x, n - 1, x.ndim - 1))


COL = ((1, 2, 0, None), (0, 1, None, 2))


def paired(tap, order):
    lines = []
    for ro in range(2):
        for po in range(2):
            line = []
            for ri in range(4):
                a = ri - ro
                for v, lo, hi in order:
                    b = COL[po][v]
                    if b is None or not 0 <= a < 3:
                        line.append(jnp.zeros((tap[0].shape[0], hi - lo), tap[0].dtype))
                    else:
                        line.append(tap[3 * a + b][:, lo:hi])
            lines.append(jnp.concatenate(line, axis=1))
    return lines


def weights_kernel(heads, first_ref, second_ref, down_ref, coarse_ref, key_ref, out_ref, dec_ref, w1_ref, w2_ref, wd_ref, wc_ref, kw_ref, wo_ref, wdec_ref):
    fine_ch = second_ref.shape[1]
    coarse_ch = coarse_ref.shape[1]
    bands = first_ref.shape[2]
    perm_f, perm_c = regroup_matrix(fine_ch, heads), regroup_matrix(coarse_ch, heads)
    perm_k = regroup_matrix(key_ref.shape[0], heads)

    def right(w, perm):
        return lax.dot_general(w, perm, (((1,), (1,)), ((), ())), preferred_element_type=F32)

    row = lax.broadcasted_iota(jnp.int32, (bands, 256), 0)
    col = lax.broadcasted_iota(jnp.int32, (bands, 256), 1)
    for ro in range(2):
        for po in range(2):
            total = jnp.zeros((fine_ch, 256), F32)
            for ri in range(4):
                for v in range(4):
                    a, b = ri - ro, COL[po][v]
                    if b is not None and 0 <= a < 3:
                        place = (col == row + (4 * ri + v) * 16).astype(F32).astype(BF)
                        total = total + dot(first_ref[3 * a + b], place)
            base = fine_ch * (2 * ro + po)
            w1_ref[base:base + fine_ch, :] = total.astype(BF)
    taps = [dot(perm_f, second_ref[k]) for k in range(9)]
    for k, line in enumerate(paired(taps, [(v, 0, fine_ch) for v in range(4)])):
        w2_ref[fine_ch * k:fine_ch * (k + 1), :] = line.astype(BF)
    wd_ref[...] = jnp.concatenate([right(down_ref[k], perm_f) for k in range(4)], axis=1).astype(BF)
    taps = [dot(perm_c, coarse_ref[k]).astype(BF) for k in range(9)]
    for ro in range(2):
        for ri in range(4):
            for v, b in enumerate((1, 0, 2)):
                a = ri - ro
                x = taps[3 * a + b] if 0 <= a < 3 else jnp.zeros((coarse_ch, coarse_ch), BF)
                base = coarse_ch * (3 * ri + v)
                wc_ref[coarse_ch * ro:coarse_ch * (ro + 1), base:base + coarse_ch] = x
    kw = right(dot(perm_k, key_ref[...]).astype(BF), perm_c).astype(BF)
    nk = kw.shape[0]
    kw_ref[...] = jnp.zeros(kw_ref.shape, BF)
    kw_ref[:nk, :coarse_ch] = kw
    kw_ref[nk:, coarse_ch:] = kw
    wo_ref[...] = right(out_ref[...], perm_c).astype(BF)
    taps = []
    for k in range(9):
        w = dec_ref[k]
        taps.append(jnp.concatenate([w[:, :fine_ch].astype(F32), right(w[:, fine_ch:], perm_f)], axis=1))
    up, skip = (0, fine_ch), (fine_ch, 2 * fine_ch)
    order = [(0, *up), (1, *up), (0, *skip), (1, *skip), (2, *up), (2, *skip), (3, *up), (3, *skip)]
    for k, line in enumerate(paired(taps, order)):
        wdec_ref[fine_ch * k:fine_ch * (k + 1), :] = line.astype(BF)


def regroup_matrix(n, heads):
    row = lax.broadcasted_iota(jnp.int32, (n, n), 0)
    col = lax.broadcasted_iota(jnp.int32, (n, n), 1)
    want = lax.rem(row, heads) * (n // heads) + lax.div(row, heads)
    return (col == want).astype(F32).astype(BF)


def regroup(w, axis, heads):
    axis = axis % w.ndim
    n = w.shape[axis] // heads
    shape = w.shape[:axis] + (heads, n) + w.shape[axis + 1:]
    return jnp.swapaxes(w.reshape(shape), axis, axis + 1).reshape(w.shape)


def encode_kernel(heads, fine_ch, coarse_ch, edge_ref, up_ref, img_ref, dn_ref, cloud_ref, order_ref, sel_ref, w1_ref, w2_ref, wd_ref, wc_ref,
                  kw_ref, kb_ref, q_ref, ml_ref, out_ref, xi, s1, s2, m_s, l_s, a_s, k_s):
    t = pl.program_id(0)
    half = xi.shape[1]
    bands = 16
    top, bottom = edge_ref[0], edge_ref[1]

    @pl.when(t == 0)
    def _():
        m_s[...] = jnp.full(m_s.shape, NEG, F32)
        l_s[...] = jnp.zeros(l_s.shape, F32)
        a_s[...] = jnp.zeros(a_s.shape, F32)
        k_s[...] = jnp.zeros(k_s.shape, F32)

    sel = sel_ref[...]
    img = jnp.concatenate([r[0].astype(F32) for r in (up_ref, img_ref, dn_ref)], axis=0).astype(BF)
    img = dot(order_ref[...], img).astype(BF)
    es, os = [], []
    for q in range(2 * half // 256):
        y = dot(img[:, 256 * q:256 * q + 256], sel)
        es.append(y[:, :128])
        os.append(y[:, 128:])
    e = jnp.concatenate(es, axis=1)
    o = jnp.concatenate(os, axis=1)
    variants = (e, o, from_left(o), from_right(e))
    for v, x in enumerate(variants):
        x = x.astype(BF)
        for r in range(12):
            xi[64 * r + bands * v:64 * r + bands * v + bands, :] = x[bands * r:bands * r + bands]
    for g in range(5):
        y = dot(w1_ref[...], xi[128 * g:128 * g + 256, :])
        y = act(y.reshape(4, fine_ch, half))
        for ro in range(2):
            k = 2 * g + ro
            e, o = y[2 * ro], y[2 * ro + 1]
            if k < 3:
                e, o = e * top, o * top
            if k > 6:
                e, o = e * bottom, o * bottom
            base = 4 * fine_ch * k
            for v, x in enumerate((e, o, from_left(o), from_right(e))):
                s1[base + fine_ch * v:base + fine_ch * (v + 1), :] = x.astype(BF)
    fines = []
    for g in range(4):
        w = w2_ref[:2 * fine_ch, :12 * fine_ch]
        at = 8 * fine_ch * g
        y = jnp.concatenate([dot(w, s1[at + 4 * fine_ch * k:at + 4 * fine_ch * (k + 3), :]) for k in range(2)], axis=0)
        f = act(y.reshape(4, fine_ch, half)).reshape(4 * fine_ch, half).astype(BF)
        if g in (1, 2):
            fines.append(f)
        low = act(dot(wd_ref[...], f)[None])[0]
        if g == 0:
            low = low * top
        if g == 3:
            low = low * bottom
        base = 3 * coarse_ch * g
        for v, x in enumerate((low, from_left(low), from_right(low))):
            s2[base + coarse_ch * v:base + coarse_ch * (v + 1), :] = x.astype(BF)
    y = dot(wc_ref[...], s2[...])
    coarse = act(y.reshape(2, coarse_ch, half)).reshape(2 * coarse_ch, half).astype(BF)
    km = (dot(kw_ref[...], coarse) + kb_ref[0]) * q_ref[...]
    km = km.reshape(2, km.shape[0] // (2 * heads), heads, half)
    scores = 0.5 * jnp.sum(km, axis=1)
    for rr in range(2):
        valid = cloud_ref[0, rr:rr + 1, :] == 1
        s = jnp.where(valid, scores[rr], NEG)
        m_old = m_s[rr]
        m_new = jnp.maximum(m_old, s)
        f = jnp.exp(m_old - m_new)
        p = jnp.where(valid, jnp.exp(s - m_new), 0.0)
        m_s[rr] = m_new
        l_s[rr] = l_s[rr] * f + p
        c = coarse[coarse_ch * rr:coarse_ch * (rr + 1)].reshape(-1, heads, half).astype(F32)
        a_s[rr] = a_s[rr] * f[None] + p[None] * c
        c = fines[rr].reshape(-1, heads, half).astype(F32)
        k_s[rr] = k_s[rr] * f[None] + p[None] * c

    @pl.when(t == pl.num_programs(0) - 1)
    def _():
        for rr in range(2):
            total = l_s[rr]
            lse = m_s[rr] + jnp.log(jnp.maximum(total, 0.5))
            ml_ref[heads * rr:heads * (rr + 1), :] = jnp.where(total > 0.0, lse, NEG)
            inv = (1.0 / jnp.maximum(total, 0.5))[None]
            a = (a_s[rr] * inv).reshape(coarse_ch, half)
            out_ref[coarse_ch * rr:coarse_ch * (rr + 1), :] = a.astype(BF)
            base = 2 * coarse_ch + 4 * fine_ch * rr
            k = (k_s[rr] * inv).reshape(4 * fine_ch, half)
            out_ref[base:base + 4 * fine_ch, :] = k.astype(BF)


def tail_kernel(heads, fine_ch, coarse_ch, groups, count, starts, per, ml_ref, ab_ref, wo_ref, wu_ref, wdec_ref,
                cls_ref, bias_ref, out_ref, ml_in, ab_in, halo_out, halo_in, edge_out, edge_in, s3, send, recv, edge_send, edge_recv):
    width = ab_in.shape[2]
    n = 4 * fine_ch
    rows = out_ref.shape[1]
    packed = groups == 2 and per % 128 == 0 and width == per + 128
    me = lax.axis_index("date")
    sides = lax.axis_size("row")
    band = lax.axis_index("tile") * sides + lax.axis_index("row")
    mesh_id = pl.DeviceIdType.MESH

    def start_of(k):
        at = starts[0]
        for j in range(1, groups):
            at = at + (starts[j] - starts[j - 1]) * ((k + groups - j) // groups)
        return pl.multiple_of(at, 128)

    def beside(step):
        other = band + step
        return {"tile": other // sides, "row": other % sides}

    barrier = pltpu.get_barrier_semaphore()
    for step in range(1, groups):
        pl.semaphore_signal(barrier, inc=1, device_id={"date": (me + step) % groups}, device_id_type=mesh_id)

    @pl.when(band > 0)
    def _():
        pl.semaphore_signal(barrier, inc=1, device_id=beside(-1), device_id_type=mesh_id)

    @pl.when(band < count - 1)
    def _():
        pl.semaphore_signal(barrier, inc=1, device_id=beside(1), device_id_type=mesh_id)

    pl.semaphore_wait(barrier, groups - 1 + (band + count - 1) // count + (2 * count - 2 - band) // count)

    copies = []
    for step in range(1, groups):
        to = (me + step) % groups
        cols = pl.ds(start_of(to), width)
        pairs = [(ml_ref.at[:, cols], ml_in.at[step - 1])]
        if packed:
            own = ab_ref.at[:, pl.ds(pl.multiple_of(per * to, 128), per)]
            pairs.append((own, ab_in.at[0, :, pl.ds(pl.multiple_of(128 * to, 128), per)]))
            block = ab_ref[:, pl.ds(pl.multiple_of(per - 128 + 128 * me, 128), 128)]
            lane = lax.broadcasted_iota(jnp.int32, (16, 128), 1)
            line = lax.broadcasted_iota(jnp.int32, (16, 128), 0)
            mark = ((line == 0) & (lane == 127 * (1 - me))).astype(F32).astype(BF)
            halo_out[...] = lax.dot_general(
                mark, block, (((1,), (1,)), ((), ())), preferred_element_type=F32).astype(BF)
            pairs.append((halo_out, halo_in))
        else:
            pairs.append((ab_ref.at[:, cols], ab_in.at[step - 1]))
        for kind, (src, dst) in enumerate(pairs):
            at = 3 * (step - 1) + kind
            copies.append(pltpu.make_async_remote_copy(
                src_ref=src, dst_ref=dst, send_sem=send.at[at], recv_sem=recv.at[at],
                device_id={"date": to}, device_id_type=mesh_id))
            copies[-1].start()
    mine = start_of(me)
    cols = pl.ds(mine, width)
    src = lax.broadcasted_iota(jnp.int32, (2 * width, out_ref.shape[2]), 0)
    dst = lax.broadcasted_iota(jnp.int32, (2 * width, out_ref.shape[2]), 1)
    pick = src == me * per - mine + lax.shift_right_logical(dst, 1) + (dst & 1) * width
    pick = pick.astype(F32).astype(BF)
    for copy in copies:
        copy.wait()
    if packed:
        lane = lax.broadcasted_iota(jnp.int32, (16, 128), 1)
        line = lax.broadcasted_iota(jnp.int32, (16, 128), 0)
        mark = ((line == 0) & (lane == 127 * me)).astype(F32).astype(BF)
        block = lax.dot_general(halo_in[...], mark, (((0,), (0,)), ((), ())), preferred_element_type=F32)
        ab_in[0, :, pl.ds(pl.multiple_of(per * (1 - me), 128), 128)] = block.astype(BF)

    def put(k, x):
        base = 2 * n * k
        half = 2 * fine_ch
        s3[base:base + n, :] = x
        x = x.astype(F32).reshape(2, 2, fine_ch, width)
        s3[base + n:base + n + half, :] = from_left(x[:, 1].reshape(half, width)).astype(BF)
        s3[base + n + half:base + 2 * n, :] = from_right(x[:, 0].reshape(half, width)).astype(BF)

    joined = []
    for rr in range(2):
        head = slice(heads * rr, heads * (rr + 1))
        ms = [ml_ref[head, cols]] + [ml_in[d, head, :] for d in range(groups - 1)]
        top = functools.reduce(jnp.maximum, ms)
        ws = [jnp.exp(m - top) for m in ms]
        inv = 1.0 / functools.reduce(jnp.add, ws)
        ws = [(w * inv)[None] for w in ws]

        def mix(base, size):
            parts = [ab_ref[base:base + size, cols]] + [ab_in[d, base:base + size, :] for d in range(groups - 1)]
            parts = [w * x.reshape(-1, heads, width).astype(F32) for w, x in zip(ws, parts)]
            return functools.reduce(jnp.add, parts).reshape(size, width).astype(BF)

        agg = mix(coarse_ch * rr, coarse_ch)
        skip = mix(2 * coarse_ch + n * rr, n)
        co = act(dot(wo_ref[...], agg)[None])[0].astype(BF)
        up = dot(wu_ref[...], co).astype(BF)
        half = 2 * fine_ch
        for a in range(2):
            joined.append(jnp.concatenate([up[half * a:half * (a + 1)], skip[half * a:half * (a + 1)]], axis=0))
    edge_out[0] = joined[0]
    edge_out[1] = joined[rows - 1]
    above = pltpu.make_async_remote_copy(
        src_ref=edge_out.at[0], dst_ref=edge_in.at[1], send_sem=edge_send.at[0], recv_sem=edge_recv.at[1],
        device_id=beside(-1), device_id_type=mesh_id)
    below = pltpu.make_async_remote_copy(
        src_ref=edge_out.at[1], dst_ref=edge_in.at[0], send_sem=edge_send.at[1], recv_sem=edge_recv.at[0],
        device_id=beside(1), device_id_type=mesh_id)

    @pl.when(band > 0)
    def _():
        above.start()

    @pl.when(band < count - 1)
    def _():
        below.start()

    for k, x in enumerate(joined):
        put(k + 1, x)

    @pl.when(band > 0)
    def _():
        above.wait_send()
        below.wait_recv()

    @pl.when(band == 0)
    def _():
        edge_in[0] = jnp.zeros((n, width), BF)

    @pl.when(band < count - 1)
    def _():
        below.wait_send()
        above.wait_recv()

    @pl.when(band == count - 1)
    def _():
        edge_in[1] = jnp.zeros((n, width), BF)

    put(0, edge_in[0])
    put(rows + 1, edge_in[1])
    for g in range(rows // 2):
        y = dot(wdec_ref[...], s3[4 * n * g:4 * n * g + 8 * n, :])
        y = act(y.reshape(4, fine_ch, width)).astype(BF)
        for ro in range(2):
            d = jnp.concatenate([y[2 * ro], y[2 * ro + 1]], axis=1)
            d = dot(d, pick).astype(BF)
            out_ref[:, 2 * g + ro, :] = dot(cls_ref[...], d) + bias_ref[...]


VMEM = pl.BlockSpec(memory_space=pltpu.VMEM)
SMEM = pl.BlockSpec(memory_space=pltpu.SMEM)


def neighbour_shift(x, step):
    count = lax.axis_size(ROWS)
    if step > 0:
        pairs = [(i, i + 1) for i in range(count - 1)]
    else:
        pairs = [(i + 1, i) for i in range(count - 1)]
    return lax.ppermute(x, ROWS, pairs)


def body(images, clouds, day_of_year, conv_first, conv_second, conv_down, conv_coarse, key_weight, query_weight,
         out_weight, up_weight, dec_weight, cls_weight, cls_bias):
    dates, bands, rows, cols = images.shape
    half = cols // 2
    fine_ch = conv_second.shape[1]
    coarse_ch = conv_coarse.shape[1]
    heads, key_size = query_weight.shape
    classes = cls_weight.shape[0]
    groups = lax.axis_size("date")
    band = lax.axis_index(ROWS)
    count = lax.axis_size(ROWS)

    flat = images.reshape(dates, bands * rows, cols)
    above = neighbour_shift(flat, 1)
    below = neighbour_shift(flat, -1)
    order = np.zeros((12 * 16, 3 * bands * rows), np.float32)
    for k in range(3):
        for r in range(rows):
            for c in range(bands):
                order[(rows * k + r) * 16 + c, (bands * k + c) * rows + r] = 1
    order = jnp.asarray(order, BF)

    edges = jnp.stack([(band > 0).astype(F32), (band < count - 1).astype(F32)])

    sel = np.zeros((256, 256), np.float32)
    for i in range(128):
        sel[2 * i, i] = 1
        sel[2 * i + 1, 128 + i] = 1
    sel = jnp.asarray(sel, BF)

    nk = 2 * heads * key_size
    n = 4 * fine_ch
    const = lambda *shape: pl.BlockSpec(shape, lambda t: (0,) * len(shape))
    raw = (conv_first, conv_second, conv_down, conv_coarse, key_weight, out_weight, dec_weight)
    shapes = [(n, 256), (n, 16 * fine_ch), (coarse_ch, n), (2 * coarse_ch, 12 * coarse_ch), (nk, 2 * coarse_ch),
              (coarse_ch, coarse_ch), (n, 8 * n)]
    w1, w2, wd, wc, kw2, wo, wdec = pl.pallas_call(
        functools.partial(weights_kernel, heads),
        grid=(1,),
        in_specs=[const(*w.shape) for w in raw],
        out_specs=[const(*shape) for shape in shapes],
        out_shape=[jax.ShapeDtypeStruct(shape, BF) for shape in shapes],
        compiler_params=pltpu.CompilerParams(vmem_limit_bytes=48 * 1024 * 1024),
        cost_estimate=pl.CostEstimate(flops=10**9, bytes_accessed=6 * 10**6, transcendentals=0),
    )(*raw)

    half_ch = coarse_ch // 2
    freqs = jnp.power(1000.0, -2.0 * jnp.arange(half_ch, dtype=F32) / coarse_ch)
    angles = day_of_year.astype(F32)[:, None] * freqs[None, :]
    encoding = jnp.concatenate([jnp.sin(angles), jnp.cos(angles)], axis=1)
    kb = jnp.dot(encoding, key_weight.astype(F32).T, precision=lax.Precision.HIGHEST)
    kb = regroup(kb, 1, heads)
    kb = jnp.concatenate([kb, kb], axis=1)[:, :, None]
    qv = jnp.transpose(query_weight).reshape(-1)
    qv = jnp.concatenate([qv, qv])[:, None]

    total = 2 * coarse_ch + 8 * fine_ch
    ml, ab = pl.pallas_call(
        functools.partial(encode_kernel, heads, fine_ch, coarse_ch),
        grid=(dates,),
        in_specs=[
            SMEM,
            *[pl.BlockSpec((1, bands * rows, cols), lambda t: (t, 0, 0))] * 3,
            pl.BlockSpec((1, 2, half), lambda t: (t, 0, 0)),
            const(*order.shape),
            const(256, 256),
            const(*w1.shape),
            const(*w2.shape),
            const(*wd.shape),
            const(*wc.shape),
            const(*kw2.shape),
            pl.BlockSpec((1, nk, 1), lambda t: (t, 0, 0)),
            const(nk, 1),
        ],
        out_specs=[const(2 * heads, half), const(total, half)],
        out_shape=[jax.ShapeDtypeStruct((2 * heads, half), F32), jax.ShapeDtypeStruct((total, half), BF)],
        scratch_shapes=[
            pltpu.VMEM((12 * 64, half), BF),
            pltpu.VMEM((40 * fine_ch, half), BF),
            pltpu.VMEM((12 * coarse_ch, half), BF),
            pltpu.VMEM((2, heads, half), F32),
            pltpu.VMEM((2, heads, half), F32),
            pltpu.VMEM((2, coarse_ch // heads, heads, half), F32),
            pltpu.VMEM((2, 4 * fine_ch // heads, heads, half), F32),
        ],
        compiler_params=pltpu.CompilerParams(vmem_limit_bytes=48 * 1024 * 1024),
    )(edges, above, flat, below, clouds, order, sel, w1, w2, wd, wc, kw2, kb, qv)

    per = half // groups
    spans = []
    for k in range(groups):
        lo = max(0, (k * per - 1) // 128)
        hi = min(half // 128 - 1, (k * per + per) // 128)
        spans.append((lo, hi))
    width = max(hi - lo + 1 for lo, hi in spans) * 128
    starts = [min(lo * 128, half - width) for lo, hi in spans]
    return pl.pallas_call(
        functools.partial(tail_kernel, heads, fine_ch, coarse_ch, groups, count, starts, per),
        in_specs=[VMEM] * 7,
        out_specs=VMEM,
        out_shape=jax.ShapeDtypeStruct((classes, rows, cols // groups), F32),
        scratch_shapes=[
            pltpu.VMEM((groups - 1, 2 * heads, width), F32),
            pltpu.VMEM((groups - 1, total, width), BF),
            pltpu.VMEM((16, total), BF),
            pltpu.VMEM((16, total), BF),
            pltpu.VMEM((2, n, width), BF),
            pltpu.VMEM((2, n, width), BF),
            pltpu.VMEM(((rows + 2) * 2 * n, width), BF),
            pltpu.SemaphoreType.DMA((3 * (groups - 1),)),
            pltpu.SemaphoreType.DMA((3 * (groups - 1),)),
            pltpu.SemaphoreType.DMA((2,)),
            pltpu.SemaphoreType.DMA((2,)),
        ],
        compiler_params=pltpu.CompilerParams(
            vmem_limit_bytes=48 * 1024 * 1024, collective_id=0, has_side_effects=True),
    )(ml, ab, wo, up_weight.reshape(n, coarse_ch), wdec, cls_weight, cls_bias[:, None])


def solution(mesh):
    return jax.shard_map(
        body,
        mesh=mesh,
        in_specs=(
            P("date", None, ("grp", "tile", "row"), None),
            P("date", ("grp", "tile", "row"), None),
            P(("grp", "date")),
        ) + (P(),) * 11,
        out_specs=P(None, ("grp", "tile", "row"), "date"),
        check_vma=False,
    )
```
